32 devices in a mesh: rep: 8 (over z, x), dp: 4 (over y, core).
Axes of the slice: x: 2, y: 2, z: 4, core: 2. Of those that a mesh axis runs over, the one named last changes fastest.
Arguments:
- residual_flow: bfloat16 [1536, 1024], P('dp'), may hold values from -6 to 6
- rooted_input_matrix: bfloat16 [8, 1024, 2048], P('rep', None, 'dp'), may hold values from -6 to 6
- chain_normal_draws: bfloat16 [8, 1024, 2048], P('rep', None, 'dp'), may hold values from -6 to 6
- output_matrix: bfloat16 [2048, 1024], P('dp'), may hold values from -0.125 to 0.125
- chain_heat: float32 [8], P('rep'), may hold values from 0.05 to 1
- matched_chain: int32 [8], P('rep'), may hold values from 0 to 7, as said below
- swap_mask: int32 [8], P('rep'), may hold values from 0 to 1, as said below
Outputs:
- swapped: bfloat16 [8, 1024, 2048], P('rep', None, 'dp')
- chain_gaps: float32 [8, 2, 2048], P('rep', None, 'dp')
The draws below stay inside these ranges and needn't reach their ends.
Inputs may be any that keep to these rules, and one draw needn't show every extreme that they name: Replicas form aligned blocks of four; in each block one of these holds: 4b with 4b + 1 and 4b + 2 with 4b + 3 are mates; only 4b + 1 with 4b + 2; only 4b with 4b + 1; only 4b + 2 with 4b + 3. matched_chain[r] is r's mate, or r where r has none. `swap_mask`: mates carry the same flag; a replica without a mate carries 0; every matched pair of the first block carries 1.
All inputs are finite; a program needn't handle non-finite values.
Results may differ from the reference program's by a relative error of at most 0.014.
Values may be sent and summed in bfloat16 or wider, within the bound.
No kernel may reach another device: no remote copies, remote signals or barrier semaphores. Data moves between devices by JAX's collectives and lax.ppermute only.
A program may use at most 64 MiB of HBM per device.

```python
import math
import jax
import jax.numpy as jnp
from jax import lax

D = 1024
FF = 2048
TOK_DEV = 384
TOKENS = 1536
CHAIN_TOTAL = 8


def mating(key):
    rank = jnp.arange(CHAIN_TOTAL, dtype=jnp.int32)
    pattern = jax.random.randint(jax.random.fold_in(key, 17), (CHAIN_TOTAL // 4,), 0, 4)
    local_kind = pattern[rank // 4]
    place = rank % 4
    paired = jnp.bitwise_xor(rank, 1)
    middle = jnp.where(place == 1, rank + 1, jnp.where(place == 2, rank - 1, rank))
    lower_only = jnp.where(place < 2, paired, rank)
    upper_only = jnp.where(place >= 2, paired, rank)
    mate = jnp.where(local_kind == 0, paired, jnp.where(local_kind == 1, middle, jnp.where(local_kind == 2, lower_only, upper_only)))
    coins = jax.random.randint(jax.random.fold_in(key, 29), (CHAIN_TOTAL,), 0, 2)
    lowest = jnp.minimum(mate, rank)
    pair_coin = jnp.where(lowest // 4 == 0, 1, coins[lowest])
    flags = jnp.where(mate != rank, pair_coin, 0)
    return (mate.astype(jnp.int32), flags.astype(jnp.int32))


def draw_matched_chain(key, part):
    return mating(key)[0]


def draw_swap_mask(key, part):
    return mating(key)[1]


def level_of(own_key, dims, cuts, low, high):
    factor_of, own = 1.0, jax.random.fold_in(own_key, 6)
    for axis_at, blocks in cuts:
        heights = jnp.exp(jax.random.uniform(jax.random.fold_in(own, axis_at), (blocks,), jnp.float32, low / len(cuts), high / len(cuts)))
        factor_of = factor_of * jnp.repeat(heights, dims[axis_at] // blocks).reshape([-1 if axis == axis_at else 1 for axis in range(len(dims))])
    return factor_of


def bell_draw(stream_key, extent, scale, bound, pieces=(), kind=jnp.bfloat16):
    result = scale * jax.random.normal(stream_key, extent, jnp.float32)
    if pieces:
        result = result * level_of(stream_key, extent, pieces, -0.22, 0.18)
    return jnp.clip(result, -bound, bound).astype(kind)


def setup_inputs(seed: int = 0) -> dict:
    keys = jax.random.split(jax.random.key(seed), 8)
    residual_flow = bell_draw(keys[0], (TOKENS, D), 1.0, 6.0, ((0, 4),))
    rooted_input_matrix = bell_draw(keys[1], (CHAIN_TOTAL, D, FF), 1.0, 6.0, ((0, 8), (2, 4)))
    chain_normal_draws = bell_draw(keys[2], (CHAIN_TOTAL, D, FF), 1.0, 6.0, ((0, 8), (2, 4)))
    output_matrix = bell_draw(keys[3], (FF, D), FF ** -0.5, 0.125, ((0, 4),))
    chain_heat = jnp.clip(jnp.exp(math.log(1.0) - 2.9957323 * jax.random.uniform(keys[4], (CHAIN_TOTAL,), jnp.float32) ** level_of(keys[4], (CHAIN_TOTAL,), ((0, 8),), -0.2, 0.2)), 0.05, 1.0)
    matched_chain = draw_matched_chain(jax.random.fold_in(keys[7], 71), 0)
    swap_mask = draw_swap_mask(jax.random.fold_in(keys[7], 71), 0)
    return {"residual_flow": residual_flow, "rooted_input_matrix": rooted_input_matrix, "chain_normal_draws": chain_normal_draws, "output_matrix": output_matrix, "chain_heat": chain_heat, "matched_chain": matched_chain, "swap_mask": swap_mask}


drift_stride = 0.5

def normalize(residual_flow):
    values = residual_flow.astype(jnp.float32)
    center = values - lax.optimization_barrier(jnp.mean(values, axis=1, keepdims=True))
    spread = lax.optimization_barrier(jnp.mean(center * center, axis=1, keepdims=True))
    return (center * lax.rsqrt(spread + 1e-05)).astype(jnp.bfloat16)

def gelu_value(values):
    inner = math.sqrt(2.0 / math.pi) * (values + 0.044715 * values * values * values)
    return 0.5 * values * (1.0 + jnp.tanh(inner))

def gelu_slope(values):
    coeff = math.sqrt(2.0 / math.pi)
    inner = coeff * (values + 0.044715 * values * values * values)
    tangent = jnp.tanh(inner)
    return 0.5 * (1.0 + tangent) + 0.5 * values * (1.0 - tangent * tangent) * coeff * (1.0 + 3.0 * 0.044715 * values * values)

def reference(residual_flow, rooted_input_matrix, chain_normal_draws, output_matrix, chain_heat, matched_chain, swap_mask):
    factor = D ** (-0.5)
    normed = normalize(residual_flow)
    blocks = TOKENS // TOK_DEV
    inputs = residual_flow.astype(jnp.float32).reshape(blocks, TOK_DEV, D)

    def lone_chain(items):
        params, noise, temp = items
        preact = jnp.dot(normed, params, preferred_element_type=jnp.float32) * factor
        hidden = gelu_value(preact).astype(jnp.bfloat16)
        output = residual_flow.astype(jnp.float32) + jnp.dot(hidden, output_matrix, preferred_element_type=jnp.float32)
        output = output.reshape(blocks, TOK_DEV, D)
        errors = jnp.concatenate([output[:, :-1] - inputs[:, 1:], jnp.zeros((blocks, 1, D), jnp.float32)], axis=1)
        errors = errors.reshape(TOKENS, D).astype(jnp.bfloat16)
        hidden_grad = jnp.dot(errors, output_matrix.T, preferred_element_type=jnp.float32)
        preact_grad = (hidden_grad * gelu_slope(preact)).astype(jnp.bfloat16)
        partial_value = jnp.einsum('ktd,ktf->kdf', normed.reshape(blocks, TOK_DEV, D).astype(jnp.float32), preact_grad.reshape(blocks, TOK_DEV, FF).astype(jnp.float32)) * factor
        gradient = lax.optimization_barrier(jnp.sum(partial_value.astype(jnp.bfloat16).astype(jnp.float32), axis=0))
        current = params.astype(jnp.float32)
        moved = current - drift_stride * (gradient + current) + jnp.sqrt(2.0 * drift_stride * temp) * noise.astype(jnp.float32)
        return moved.astype(jnp.bfloat16)
    refreshed_input_matrix = lax.map(lone_chain, (rooted_input_matrix, chain_normal_draws, chain_heat))

    def gap_of(index):
        own = refreshed_input_matrix[index].astype(jnp.float32)
        below = refreshed_input_matrix[(index - 1) % CHAIN_TOTAL].astype(jnp.float32)
        above = refreshed_input_matrix[(index + 1) % CHAIN_TOTAL].astype(jnp.float32)
        lower_gap = lax.optimization_barrier(jnp.mean((own - below) * (own - below), axis=0))
        upper_gap = lax.optimization_barrier(jnp.mean((own - above) * (own - above), axis=0))
        return jnp.stack([lower_gap, upper_gap], axis=0)
    chain_gaps = lax.map(gap_of, jnp.arange(CHAIN_TOTAL, dtype=jnp.int32))
    taken = (swap_mask == 1)[:, None, None]
    swapped = jnp.where(taken, refreshed_input_matrix[matched_chain.astype(jnp.int32)], refreshed_input_matrix)
    return (swapped, chain_gaps)
```

```python
import functools
import math

import jax
import jax.numpy as jnp
from jax import lax
from jax.experimental import pallas as pl
from jax.experimental.pallas import tpu as pltpu
from jax.sharding import PartitionSpec as P

drift_stride = 0.5
lanes = 128
f32 = jnp.float32
bf16 = jnp.bfloat16
limit = pltpu.CompilerParams(vmem_limit_bytes=40 * 1024 * 1024)
smem = pl.BlockSpec(memory_space=pltpu.SMEM)


def matmul(left, right):
    return jnp.dot(left, right, preferred_element_type=f32)


def against_rows(left, right):
    return lax.dot_general(left, right, (((1,), (1,)), ((), ())), preferred_element_type=f32)


def cost(macs, nbytes):
    return pl.CostEstimate(flops=2 * macs, bytes_accessed=nbytes, transcendentals=0)


def whole(array):
    rank = array.ndim
    return pl.BlockSpec(array.shape, lambda *_: (0,) * rank)


def shape(dims, dtype=bf16):
    return jax.ShapeDtypeStruct(dims, dtype)


def assemble_kernel(place_ref, own, across, behind, upper, lower, out):
    rows = own.shape[0]
    half = rows // 2
    for place in range(4):

        @pl.when(place_ref[0] == place)
        def _():
            out[place * rows : (place + 1) * rows] = own[...]
            out[(place ^ 1) * rows : ((place ^ 1) + 1) * rows] = across[...]
            out[(place ^ 2) * rows : ((place ^ 2) + 1) * rows] = behind[...]
            out[(place ^ 3) * rows : (place ^ 3) * rows + half] = upper[...]
            out[(place ^ 3) * rows + half : ((place ^ 3) + 1) * rows] = lower[...]


def assemble(place, pieces):
    rows, width = pieces[0].shape
    return pl.pallas_call(
        assemble_kernel,
        grid=(1,),
        out_shape=shape((4 * rows, width)),
        in_specs=[smem] + [whole(piece) for piece in pieces],
        out_specs=pl.BlockSpec((4 * rows, width), lambda *_: (0, 0)),
        compiler_params=limit,
        cost_estimate=cost(0, 16 * rows * width),
    )(place, *pieces)


def forward_kernel(tokens, own_in, mate_in, own_out, mate_out, normed_t, slope, first, second, normed, total):
    step = pl.program_id(0)
    steps = pl.num_programs(0)
    width = tokens.shape[1]

    @pl.when(step == 0)
    def _():
        values = tokens[...].astype(f32)
        center = values - jnp.mean(values, axis=1, keepdims=True)
        spread = jnp.mean(center * center, axis=1, keepdims=True)
        scaled = (center * lax.rsqrt(spread + 1e-05)).astype(bf16)
        normed[...] = scaled
        total[...] = jnp.zeros_like(total)

    def part(weight_in, weight_out):
        values = matmul(normed[...], weight_in[...]) * (width**-0.5)
        coeff = math.sqrt(2.0 / math.pi)
        square = values * values
        gate = 0.5 + 0.5 * jnp.tanh(coeff * values * (1.0 + 0.044715 * square))
        hidden = values * gate
        slope[0] = (
            gate + hidden * (1.0 - gate) * (2.0 * coeff + 6.0 * 0.044715 * coeff * square)
        ).astype(bf16)
        total[...] += matmul(hidden.astype(bf16), weight_out[...])

    @pl.when(step < steps // 2)
    def _():
        part(own_in, own_out)

    @pl.when(step >= steps // 2)
    def _():
        part(mate_in, mate_out)

    @pl.when(step == steps - 1)
    def _():
        half = first.shape[0]
        first[...] = total[:half].astype(bf16)
        second[...] = total[half:].astype(bf16)
        normed_t[...] = normed[...].T


def forward(tokens, own_in, mate_in, own_out, mate_out):
    count, width = tokens.shape
    block = own_in.shape[1]
    tile = block // 2
    per = block // tile
    early = lambda step: jnp.minimum(step, per - 1)
    late = lambda step: jnp.maximum(step - per, 0)
    return pl.pallas_call(
        forward_kernel,
        grid=(2 * per,),
        out_shape=(
            shape((width, count)),
            shape((2, count, block)),
            shape((count // 2, width)),
            shape((count // 2, width)),
        ),
        in_specs=[
            whole(tokens),
            pl.BlockSpec((width, tile), lambda step: (0, early(step))),
            pl.BlockSpec((width, tile), lambda step: (0, late(step))),
            pl.BlockSpec((tile, width), lambda step: (early(step), 0)),
            pl.BlockSpec((tile, width), lambda step: (late(step), 0)),
        ],
        out_specs=(
            pl.BlockSpec((width, count), lambda step: (0, 0)),
            pl.BlockSpec((1, count, tile), lambda step: (step // per, 0, step % per)),
            pl.BlockSpec((count // 2, width), lambda step: (0, 0)),
            pl.BlockSpec((count // 2, width), lambda step: (0, 0)),
        ),
        scratch_shapes=[pltpu.VMEM((count, width), bf16), pltpu.VMEM((count, width), f32)],
        compiler_params=limit,
        cost_estimate=cost(4 * count * width * block, 8 * width * block),
    )(tokens, own_in, mate_in, own_out, mate_out)


def errors_kernel(last, tokens, own_part, sent_part, weight, weight_mate, errors, grads):
    count = errors.shape[0]
    base = tokens.shape[0] - count if last else 0
    span = count if last else count + 16
    values = tokens[base : base + span].astype(f32)
    ahead = pltpu.roll(values, span - 1, 0)[:count]
    result = values[:count] + own_part[...].astype(f32) + sent_part[...].astype(f32) - ahead
    if last:
        rank = lax.broadcasted_iota(jnp.int32, result.shape, 0)
        result = jnp.where(rank == count - 1, 0.0, result)
    result = result.astype(bf16)
    errors[...] = result
    grads[:, :lanes] = against_rows(result, weight[...]).astype(bf16)
    grads[:, lanes:] = against_rows(result, weight_mate[...]).astype(bf16)


def errors_of(last, tokens, own_part, sent_part, weight, weight_mate):
    count, width = own_part.shape
    rows = pl.BlockSpec((lanes, width), lambda *_: (0, 0))
    return pl.pallas_call(
        functools.partial(errors_kernel, last),
        grid=(1,),
        out_shape=(shape((count, width)), shape((count, 2 * lanes))),
        in_specs=[whole(tokens), whole(own_part), whole(sent_part), rows, rows],
        out_specs=(
            pl.BlockSpec((count, width), lambda *_: (0, 0)),
            pl.BlockSpec((count, 2 * lanes), lambda *_: (0, 0)),
        ),
        compiler_params=limit,
        cost_estimate=cost(2 * count * width * lanes, 10 * count * width),
    )(tokens, own_part, sent_part, weight, weight_mate)


def away_kernel(first, second, weight, weight_mate, grads):
    half = first.shape[0]
    for at, errors in ((0, first), (half, second)):
        grads[at : at + half, :lanes] = against_rows(errors[...], weight[...]).astype(bf16)
        grads[at : at + half, lanes:] = against_rows(errors[...], weight_mate[...]).astype(bf16)


def away(chunk, first, second, weight, weight_mate):
    half, width = first.shape
    rows = pl.BlockSpec((lanes, width), lambda *_: (chunk, 0))
    return pl.pallas_call(
        away_kernel,
        grid=(1,),
        out_shape=shape((2 * half, 2 * lanes)),
        in_specs=[whole(first), whole(second), rows, rows],
        out_specs=pl.BlockSpec((2 * half, 2 * lanes), lambda *_: (0, 0)),
        compiler_params=limit,
        cost_estimate=cost(4 * half * width * lanes, 8 * half * width),
    )(first, second, weight, weight_mate)


def home_kernel(first, second, weight, weight_mate, slope, grads):
    half = first.shape[0]
    for at, errors in ((0, first), (half, second)):
        for side, rows in ((0, weight), (1, weight_mate)):
            product = against_rows(errors[...], rows[...]) * slope[side, at : at + half].astype(f32)
            grads[0, at : at + half, side * lanes : (side + 1) * lanes] = product.astype(bf16)


def home(first, second, weight, weight_mate, slope):
    half, width = first.shape
    chunks = weight.shape[0] // lanes
    rows = pl.BlockSpec((lanes, width), lambda chunk: (chunk, 0))
    return pl.pallas_call(
        home_kernel,
        grid=(chunks,),
        out_shape=shape((chunks, 2 * half, 2 * lanes)),
        in_specs=[
            whole(first),
            whole(second),
            rows,
            rows,
            pl.BlockSpec((2, 2 * half, lanes), lambda chunk: (0, 0, chunk)),
        ],
        out_specs=pl.BlockSpec((1, 2 * half, 2 * lanes), lambda chunk: (chunk, 0, 0)),
        compiler_params=limit,
        cost_estimate=cost(4 * chunks * half * width * lanes, 10 * half * width),
    )(first, second, weight, weight_mate, slope)


def gradient_kernel(parts, *refs):
    arrived = refs[:parts]
    slope, near, normed_a, normed_b, keep, send, mixed = refs[parts:]
    factor = normed_a.shape[0] ** -0.5
    count = arrived[0].shape[0]
    for part in range(parts):
        rows = slice(part * count, (part + 1) * count)
        for side in range(2):
            cols = slice(side * lanes, (side + 1) * lanes)
            mixed[rows, cols] = (
                arrived[part][:, cols].astype(f32) * slope[side, rows].astype(f32)
            ).astype(bf16)
    total = (matmul(normed_a[...], mixed[...]) + matmul(normed_b[...], near[0])) * factor
    keep[...] = total[:, :lanes]
    send[...] = total[:, lanes:].astype(bf16)


def gradient(chunk, arrived, slope, near, normed_a, normed_b):
    width, count = normed_a.shape
    return pl.pallas_call(
        functools.partial(gradient_kernel, len(arrived)),
        grid=(1,),
        out_shape=(shape((width, lanes), f32), shape((width, lanes))),
        in_specs=[whole(piece) for piece in arrived]
        + [
            pl.BlockSpec((2, count, lanes), lambda *_: (0, 0, chunk)),
            pl.BlockSpec((1, count, 2 * lanes), lambda *_: (chunk, 0, 0)),
            whole(normed_a),
            whole(normed_b),
        ],
        out_specs=(
            pl.BlockSpec((width, lanes), lambda *_: (0, 0)),
            pl.BlockSpec((width, lanes), lambda *_: (0, 0)),
        ),
        scratch_shapes=[pltpu.VMEM((count, 2 * lanes), bf16)],
        compiler_params=limit,
        cost_estimate=cost(4 * width * count * lanes, 4 * width * count),
    )(*arrived, slope, near, normed_a, normed_b)


def update_kernel(heat, keep, sent, params, noise, out):
    current = params[0].astype(f32)
    slope = keep[...] + sent[...].astype(f32)
    moved = current - drift_stride * (slope + current) + heat[0] * noise[0].astype(f32)
    out[...] = moved.astype(bf16)


def update(chunk, heat, keep, sent, params, noise):
    width = keep.shape[0]
    cols = pl.BlockSpec((1, width, lanes), lambda *_: (0, 0, chunk))
    return pl.pallas_call(
        update_kernel,
        grid=(1,),
        out_shape=shape((width, lanes)),
        in_specs=[smem, whole(keep), whole(sent), cols, cols],
        out_specs=pl.BlockSpec((width, lanes), lambda *_: (0, 0)),
        compiler_params=limit,
        cost_estimate=cost(0, 12 * width * lanes),
    )(heat, keep, sent, params, noise)


def finish_kernel(count, start, *refs):
    taken = refs[0]
    own, across, beyond = (refs[1 + i * count : 1 + (i + 1) * count] for i in range(3))
    result, gaps = refs[-2], refs[-1]
    odd = taken[0] == 1
    for at in range(count):
        cols = slice(at * lanes, (at + 1) * lanes)
        mine = own[at][...]
        near = across[at][...]
        far = beyond[at][...]
        result[0, :, cols] = jnp.where(taken[1] == 1, near, jnp.where(taken[2] == 1, far, mine))
        mine = mine.astype(f32)
        near = near.astype(f32) - mine
        far = far.astype(f32) - mine
        near = jnp.mean(near * near, axis=0, keepdims=True)
        far = jnp.mean(far * far, axis=0, keepdims=True)
        gaps[0, 0:1, cols] = jnp.where(odd, near, far)
        gaps[0, 1:2, cols] = jnp.where(odd, far, near)


def finish(start, chunks, block, flags, own, across, beyond, so_far):
    count = len(own)
    width = own[0].shape[0]
    anywhere = pl.BlockSpec(memory_space=pl.ANY)
    given = list(so_far) if so_far is not None else []
    extra = len(given)
    step = start // count

    def kernel(*refs):
        data = refs[: 1 + 3 * count]
        finish_kernel(count, start, *data, refs[-2], refs[-1])

    return pl.pallas_call(
        kernel,
        grid=(1,),
        out_shape=(shape((1, width, block)), shape((1, 2, block), f32)),
        in_specs=[smem]
        + [whole(piece) for piece in (*own, *across, *beyond)]
        + [anywhere] * extra,
        out_specs=(
            pl.BlockSpec((1, width, count * lanes), lambda *_: (0, 0, step)),
            pl.BlockSpec((1, 2, count * lanes), lambda *_: (0, 0, step)),
        ),
        input_output_aliases={1 + 3 * count + i: i for i in range(extra)},
        compiler_params=limit,
        cost_estimate=cost(0, 8 * width * lanes * count),
    )(flags, *own, *across, *beyond, *given)


def body(
    residual_flow,
    rooted_input_matrix,
    chain_normal_draws,
    output_matrix,
    chain_heat,
    matched_chain,
    swap_mask,
):
    replicas = lax.axis_size("rep")
    rank = lax.axis_index("rep")
    place = rank % 4
    params = rooted_input_matrix[0]
    block = params.shape[1]
    count = residual_flow.shape[0]

    def to_core(value):
        return lax.ppermute(value, "dp", [(i, i ^ 1) for i in range(4)])

    def to_chip(value):
        return lax.ppermute(value, "dp", [(i, i ^ 2) for i in range(4)])

    def to_mate(value):
        return lax.ppermute(value, "rep", [(i, i ^ 1) for i in range(replicas)])

    def to_pair(value):
        return lax.ppermute(value, "rep", [(i, i ^ 2) for i in range(replicas)])

    def to_next(value):
        pairs = [(i, (i + (2 if i % 2 == 0 else -2)) % replicas) for i in range(replicas)]
        return lax.ppermute(value, "rep", pairs)

    def spread(value):
        rows = value.shape[0] // 4
        own = to_chip(lax.dynamic_slice_in_dim(value, place * rows, rows, 0))
        across = to_mate(own)
        behind = to_pair(own)
        upper = to_mate(behind[: rows // 2])
        lower = to_pair(across[rows // 2 :])
        return assemble(place.astype(jnp.int32)[None], (own, across, behind, upper, lower))

    mate_in = to_core(params)
    mate_out = to_core(output_matrix)
    far_tokens = spread(residual_flow)
    far_out = spread(output_matrix)
    far_out_mate = to_core(far_out)

    normed_a, slope_a, *sent_a = forward(residual_flow, params, mate_in, output_matrix, mate_out)
    first_sum = to_chip(sent_a[0])
    second_sum = to_chip(sent_a[1])
    normed_b, slope_b, *part_b = forward(far_tokens, params, mate_in, output_matrix, mate_out)

    first_errors, first_grads = errors_of(
        False, far_tokens, part_b[0], first_sum, far_out, far_out_mate
    )
    first_grads = to_chip(first_grads)
    second_errors, second_grads = errors_of(
        True, far_tokens, part_b[1], second_sum, far_out, far_out_mate
    )
    second_grads = to_chip(second_grads)
    arrived = [(first_grads, second_grads)]
    chunks = block // lanes
    for chunk in range(1, chunks):
        arrived.append((to_chip(away(chunk, first_errors, second_errors, far_out, far_out_mate)),))
    near = home(first_errors, second_errors, output_matrix, mate_out, slope_b)

    heat = jnp.sqrt(2.0 * drift_stride * chain_heat)
    taken = swap_mask[0] == 1
    across_rank = rank ^ 1
    odd = rank % 2
    beyond_rank = jnp.where(odd == 1, rank + 1, rank - 1)
    flags = jnp.stack(
        [odd, taken & (matched_chain[0] == across_rank), taken & (matched_chain[0] == beyond_rank)]
    ).astype(jnp.int32)

    own, across, beyond = [], [], []
    for chunk in range(chunks):
        keep, send = gradient(chunk, arrived[chunk], slope_a, near, normed_a, normed_b)
        fresh = update(chunk, heat, keep, to_core(send), rooted_input_matrix, chain_normal_draws)
        own.append(fresh)
        across.append(to_mate(fresh))
        beyond.append(to_next(across[-1]))
    done = None
    for start, stop in ((0, 2), (2, 3), (3, 4)):
        done = finish(
            start, chunks, block, flags, own[start:stop], across[start:stop], beyond[start:stop], done
        )
    return done


def solution(mesh):
    placed = (
        P("dp", None),
        P("rep", None, "dp"),
        P("rep", None, "dp"),
        P("dp", None),
        P("rep"),
        P("rep"),
        P("rep"),
    )
    return jax.shard_map(
        body,
        mesh=mesh,
        in_specs=placed,
        out_specs=(P("rep", None, "dp"), P("rep", None, "dp")),
        check_vma=False,
    )
```

```python
import functools
import math

import jax
import jax.numpy as jnp
from jax import lax
from jax.experimental import pallas as pl
from jax.experimental.pallas import tpu as pltpu
from jax.sharding import PartitionSpec as P

drift_stride = 0.5
lanes = 128
f32 = jnp.float32
bf16 = jnp.bfloat16
smem = pl.BlockSpec(memory_space=pltpu.SMEM)


def matmul(left, right):
    return jnp.dot(left, right, preferred_element_type=f32)


def against_rows(left, right):
    return lax.dot_general(left, right, (((1,), (1,)), ((), ())), preferred_element_type=f32)


def limit(mebibytes):
    return pltpu.CompilerParams(vmem_limit_bytes=mebibytes * 1024 * 1024)


def cost(macs, nbytes):
    return pl.CostEstimate(flops=2 * macs, bytes_accessed=nbytes, transcendentals=0)


def whole(array):
    rank = array.ndim
    return pl.BlockSpec(array.shape, lambda *_: (0,) * rank)


def shape(dims, dtype=bf16):
    return jax.ShapeDtypeStruct(dims, dtype)


def after(value, *earlier):
    anywhere = pl.BlockSpec(memory_space=pl.ANY)
    return pl.pallas_call(
        lambda *refs: None,
        out_shape=shape(value.shape, value.dtype),
        in_specs=[anywhere] * (1 + len(earlier)),
        out_specs=anywhere,
        input_output_aliases={0: 0},
        compiler_params=limit(1),
    )(value, *earlier)


def shares_kernel(place, tokens, weight, token_share, weight_share):
    token_share[...] = tokens[...]
    weight_share[...] = weight[...]


def shares(place, tokens, weight):
    sizes = [(value.shape[0] // 4, value.shape[1]) for value in (tokens, weight)]
    return pl.pallas_call(
        shares_kernel,
        out_shape=[shape(size) for size in sizes],
        grid_spec=pltpu.PrefetchScalarGridSpec(
            num_scalar_prefetch=1,
            grid=(1,),
            in_specs=[pl.BlockSpec(size, lambda _, place: (place[0], 0)) for size in sizes],
            out_specs=[pl.BlockSpec(size, lambda *_: (0, 0)) for size in sizes],
        ),
        compiler_params=limit(3),
        cost_estimate=cost(0, 4 * sizes[0][0] * sizes[0][1]),
    )(place, tokens, weight)


def assemble_kernel(place_ref, own, across, behind, upper, lower, out):
    rows = own.shape[0]
    half = rows // 2
    for place in range(4):

        @pl.when(place_ref[0] == place)
        def _():
            out[place * rows : (place + 1) * rows] = own[...]
            out[(place ^ 1) * rows : ((place ^ 1) + 1) * rows] = across[...]
            out[(place ^ 2) * rows : ((place ^ 2) + 1) * rows] = behind[...]
            out[(place ^ 3) * rows : (place ^ 3) * rows + half] = upper[...]
            out[(place ^ 3) * rows + half : ((place ^ 3) + 1) * rows] = lower[...]


def assemble(place, pieces):
    rows, width = pieces[0].shape
    return pl.pallas_call(
        assemble_kernel,
        grid=(1,),
        out_shape=shape((4 * rows, width)),
        in_specs=[smem] + [whole(piece) for piece in pieces],
        out_specs=pl.BlockSpec((4 * rows, width), lambda *_: (0, 0)),
        compiler_params=limit(6),
        cost_estimate=cost(0, 16 * rows * width),
    )(place, *pieces)


def normalized(tokens):
    values = tokens.astype(f32)
    center = values - jnp.mean(values, axis=1, keepdims=True)
    spread = jnp.mean(center * center, axis=1, keepdims=True)
    return (center * lax.rsqrt(spread + 1e-05)).astype(bf16)


def gelu_both(values):
    coeff = math.sqrt(2.0 / math.pi)
    square = values * values
    gate = 0.5 + 0.5 * jnp.tanh(coeff * values * (1.0 + 0.044715 * square))
    hidden = values * gate
    slope = gate + hidden * (1.0 - gate) * (2.0 * coeff + 6.0 * 0.044715 * coeff * square)
    return hidden.astype(bf16), slope.astype(bf16)


def forward_core(tokens, weights_in, weights_out, normed_t, slopes, total):
    count, width = tokens.shape
    block = weights_in[0].shape[1]
    tile = min(256, block)
    normed = normalized(tokens)
    normed_t[...] = normed.T
    for side in range(2):
        for at in range(0, block, tile):
            values = matmul(normed, weights_in[side][:, at : at + tile]) * (width**-0.5)
            hidden, slopes[side][:, at : at + tile] = gelu_both(values)
            term = matmul(hidden, weights_out[side][at : at + tile])
            if side + at == 0:
                total[...] = term
            else:
                total[...] += term


def forward_kernel(tokens, own_in, mate_in, own_out, mate_out, normed_t, slope, slope_mate, out, total):
    weights = (own_in, mate_in), (own_out, mate_out)
    forward_core(tokens[...], *weights, normed_t, (slope, slope_mate), total)
    out[...] = total[...].astype(bf16)


def forward_far_kernel(place, *refs):
    pieces = refs[:5]
    own_in, mate_in, own_out, mate_out, normed_t, slope, slope_mate, out, total, tokens = refs[5:]
    assemble_kernel(place, *pieces, tokens)
    weights = (own_in, mate_in), (own_out, mate_out)
    forward_core(tokens[...], *weights, normed_t, (slope, slope_mate), total)
    count = tokens.shape[0]
    values = tokens[...].astype(f32)
    ahead = pltpu.roll(values, count - 1, 0)
    rank = lax.broadcasted_iota(jnp.int32, values.shape, 0)
    base = total[...] + values - ahead
    out[...] = jnp.where(rank == count - 1, 0.0, base)


def forward(given, count, weights, far):
    width, block = weights[0].shape
    outs = (
        shape((width, count)),
        shape((count, block)),
        shape((count, block)),
        shape((count, width), f32 if far else bf16),
    )
    scratch = [pltpu.VMEM((count, width), f32)]
    if far:
        scratch.append(pltpu.VMEM((count, width), bf16))
    return pl.pallas_call(
        forward_far_kernel if far else forward_kernel,
        grid=(1,),
        out_shape=outs,
        in_specs=[smem if value.ndim == 1 else whole(value) for value in (*given, *weights)],
        out_specs=[whole(out) for out in outs],
        scratch_shapes=scratch,
        compiler_params=limit(20),
        cost_estimate=cost(4 * count * width * block, 8 * width * block),
    )(*given, *weights)


def errors_kernel(base, sent, far, errors):
    count = errors.shape[0]
    result = base[...] + sent[...].astype(f32)
    rank = lax.broadcasted_iota(jnp.int32, result.shape, 0)
    errors[...] = jnp.where(rank == count - 1, 0.0, result).astype(bf16)


def errors_of(base, sent, far):
    return pl.pallas_call(
        errors_kernel,
        grid=(1,),
        out_shape=shape(base.shape),
        in_specs=[whole(base), whole(sent), pl.BlockSpec(memory_space=pl.ANY)],
        out_specs=whole(base),
        compiler_params=limit(8),
        cost_estimate=cost(0, 10 * base.size),
    )(base, sent, far)


def away_kernel(start, errors, errors_mate, far, *grads):
    count = errors.shape[0]
    for at, out in enumerate(grads):
        rows = slice((start + at) * lanes, (start + at + 1) * lanes)
        out[:count] = against_rows(errors[...], far[rows]).astype(bf16)
        out[count:] = against_rows(errors_mate[...], far[rows]).astype(bf16)


def away(start, stop, errors, errors_mate, far):
    count, width = errors.shape
    given = (errors, errors_mate, far)
    outs = [shape((2 * count, lanes))] * (stop - start)
    return pl.pallas_call(
        functools.partial(away_kernel, start),
        grid=(1,),
        out_shape=outs,
        in_specs=[whole(value) for value in given],
        out_specs=[whole(out) for out in outs],
        compiler_params=limit(8),
        cost_estimate=cost(2 * len(outs) * count * width * lanes, 4 * count * width),
    )(*given)


def near_kernel(errors, errors_mate, weight, slope, slope_mate, near):
    count = errors.shape[0]
    for chunk in range(near.shape[0]):
        rows = slice(chunk * lanes, (chunk + 1) * lanes)
        for at, source, factor in ((0, errors, slope), (count, errors_mate, slope_mate)):
            product = against_rows(source[...], weight[rows]) * factor[:, rows].astype(f32)
            near[chunk, at : at + count] = product.astype(bf16)


def near_of(errors, errors_mate, weight, slope, slope_mate):
    count, width = errors.shape
    chunks = weight.shape[0] // lanes
    given = (errors, errors_mate, weight, slope, slope_mate)
    out = shape((chunks, 2 * count, lanes))
    return pl.pallas_call(
        near_kernel,
        grid=(1,),
        out_shape=out,
        in_specs=[whole(value) for value in given],
        out_specs=whole(out),
        compiler_params=limit(10),
        cost_estimate=cost(2 * chunks * count * width * lanes, 10 * count * width),
    )(*given)


def update_kernel(
    heat, arrived, near, slope, slope_mate, normed, normed_mate, far, far_mate, params, noise, *rest
):
    out = rest[-1]
    width, count = normed.shape
    total = matmul(far[...], near[0, :count]) + matmul(far_mate[...], near[0, count:])
    mixed = (arrived[:count].astype(f32) * slope[...].astype(f32)).astype(bf16)
    total += matmul(normed[...], mixed)
    mixed = (arrived[count:].astype(f32) * slope_mate[...].astype(f32)).astype(bf16)
    total += matmul(normed_mate[...], mixed)
    current = params[0].astype(f32)
    moved = (
        current
        - drift_stride * (total * width**-0.5 + current)
        + heat[0] * noise[0].astype(f32)
    )
    out[...] = moved.astype(bf16)


def update(chunk, heat, arrived, near, slopes, normed, params, noise, *earlier):
    width, count = normed[0].shape
    columns = pl.BlockSpec((count, lanes), lambda *_: (0, chunk))
    block = pl.BlockSpec((1, width, lanes), lambda *_: (0, 0, chunk))
    out = shape((width, lanes))
    return pl.pallas_call(
        update_kernel,
        grid=(1,),
        out_shape=out,
        in_specs=[
            smem,
            whole(arrived),
            pl.BlockSpec((1, 2 * count, lanes), lambda *_: (chunk, 0, 0)),
            columns,
            columns,
        ]
        + [whole(value) for value in normed]
        + [block, block]
        + [pl.BlockSpec(memory_space=pl.ANY)] * len(earlier),
        out_specs=whole(out),
        compiler_params=limit(12),
        cost_estimate=cost(4 * width * count * lanes, 8 * width * count),
    )(heat, arrived, near, *slopes, *normed, params, noise, *earlier)


def finish_kernel(count, start, *refs):
    taken = refs[0]
    own, across, beyond = (refs[1 + i * count : 1 + (i + 1) * count] for i in range(3))
    result, gaps = refs[-2], refs[-1]
    odd = taken[0] == 1
    for at in range(count):
        cols = slice(at * lanes, (at + 1) * lanes)
        mine = own[at][...]
        near = across[at][...]
        far = beyond[at][...]
        result[0, :, cols] = jnp.where(taken[1] == 1, near, jnp.where(taken[2] == 1, far, mine))
        mine = mine.astype(f32)
        near = near.astype(f32) - mine
        far = far.astype(f32) - mine
        near = jnp.mean(near * near, axis=0, keepdims=True)
        far = jnp.mean(far * far, axis=0, keepdims=True)
        gaps[0, 0:1, cols] = jnp.where(odd, near, far)
        gaps[0, 1:2, cols] = jnp.where(odd, far, near)


def finish(start, chunks, block, flags, own, across, beyond, so_far):
    count = len(own)
    width = own[0].shape[0]
    anywhere = pl.BlockSpec(memory_space=pl.ANY)
    given = list(so_far) if so_far is not None else []
    extra = len(given)
    step = start // count

    def kernel(*refs):
        data = refs[: 1 + 3 * count]
        finish_kernel(count, start, *data, refs[-2], refs[-1])

    return pl.pallas_call(
        kernel,
        grid=(1,),
        out_shape=(shape((1, width, block)), shape((1, 2, block), f32)),
        in_specs=[smem]
        + [whole(piece) for piece in (*own, *across, *beyond)]
        + [anywhere] * extra,
        out_specs=(
            pl.BlockSpec((1, width, count * lanes), lambda *_: (0, 0, step)),
            pl.BlockSpec((1, 2, count * lanes), lambda *_: (0, 0, step)),
        ),
        input_output_aliases={1 + 3 * count + i: i for i in range(extra)},
        compiler_params=limit(8),
        cost_estimate=cost(0, 8 * width * lanes * count),
    )(flags, *own, *across, *beyond, *given)


def body(
    residual_flow,
    rooted_input_matrix,
    chain_normal_draws,
    output_matrix,
    chain_heat,
    matched_chain,
    swap_mask,
):
    replicas = lax.axis_size("rep")
    rank = lax.axis_index("rep")
    place = rank % 4
    params = rooted_input_matrix[0]
    block = params.shape[1]
    count = residual_flow.shape[0]

    def to_core(value):
        return lax.ppermute(value, "dp", [(i, i ^ 1) for i in range(4)])

    def to_chip(value):
        return lax.ppermute(value, "dp", [(i, i ^ 2) for i in range(4)])

    def to_mate(value):
        return lax.ppermute(value, "rep", [(i, i ^ 1) for i in range(replicas)])

    def to_pair(value):
        return lax.ppermute(value, "rep", [(i, i ^ 2) for i in range(replicas)])

    def to_next(value):
        pairs = [(i, (i + (2 if i % 2 == 0 else -2)) % replicas) for i in range(replicas)]
        return lax.ppermute(value, "rep", pairs)

    def step_one(own):
        return to_mate(own), to_pair(own)

    def step_two(own, across, behind):
        half = own.shape[0] // 2
        return own, across, behind, to_mate(behind[:half]), to_pair(across[half:])

    spot = place.astype(jnp.int32)[None]
    mate_in = to_core(params)
    mate_out = to_core(output_matrix)
    token_share, weight_share = shares(spot, residual_flow, output_matrix)
    token_own = to_chip(token_share)
    weight_own = to_chip(weight_share)
    weights = (params, mate_in, output_matrix, mate_out)
    normed, slope, slope_send, part = forward((residual_flow,), count, weights, False)
    token_own_early = token_own
    token_own = after(token_own, part)
    sent = to_chip(after(part, token_own_early))
    normed_mate = to_core(normed)
    slope_mate = to_core(slope_send)
    token_across, token_behind = step_one(token_own)
    token_pieces = step_two(token_own, token_across, token_behind)
    weight_across, weight_behind = step_one(weight_own)
    far, far_slope, far_slope_send, base = forward((spot, *token_pieces), count, weights, True)
    far_mate = to_core(far)
    far_slope_mate = to_core(far_slope_send)
    weight_across = after(weight_across, base)
    weight_pieces = step_two(weight_own, weight_across, weight_behind)
    far_out = assemble(spot, weight_pieces)

    errors = errors_of(base, sent, far_out)
    errors_mate = to_core(errors)
    chunks = block // lanes
    grads = away(0, 1, errors, errors_mate, far_out)
    grads += away(1, chunks, errors, errors_mate, far_out)
    arrived = [to_chip(value) for value in grads]
    near = near_of(errors, errors_mate, output_matrix, far_slope, far_slope_mate)

    heat = jnp.sqrt(2.0 * drift_stride * chain_heat)
    taken = swap_mask[0] == 1
    across_rank = rank ^ 1
    odd = rank % 2
    beyond_rank = jnp.where(odd == 1, rank + 1, rank - 1)
    flags = jnp.stack(
        [odd, taken & (matched_chain[0] == across_rank), taken & (matched_chain[0] == beyond_rank)]
    ).astype(jnp.int32)

    own, across, beyond = [], [], []
    for chunk in range(chunks):
        earlier = across[chunk - 2 : chunk - 1] if chunk >= 2 else own[:chunk]
        fresh = update(
            chunk,
            heat,
            arrived[chunk],
            near,
            (slope, slope_mate),
            (normed, normed_mate, far, far_mate),
            rooted_input_matrix,
            chain_normal_draws,
            *earlier,
        )
        own.append(fresh)
        across.append(to_mate(fresh))
        beyond.append(to_next(across[-1]))
    done = None
    for start, stop in ((0, 2), (2, 3), (3, 4)):
        done = finish(
            start, chunks, block, flags, own[start:stop], across[start:stop], beyond[start:stop], done
        )
    return done


def solution(mesh):
    placed = (
        P("dp", None),
        P("rep", None, "dp"),
        P("rep", None, "dp"),
        P("dp", None),
        P("rep"),
        P("rep"),
        P("rep"),
    )
    return jax.shard_map(
        body,
        mesh=mesh,
        in_specs=placed,
        out_specs=(P("rep", None, "dp"), P("rep", None, "dp")),
        check_vma=False,
    )
```

```python
import functools
import math

import jax
import jax.numpy as jnp
from jax import lax
from jax.experimental import pallas as pl
from jax.experimental.pallas import tpu as pltpu
from jax.sharding import PartitionSpec as P

drift_stride = 0.5
f32 = jnp.float32
bf16 = jnp.bfloat16
smem = pl.BlockSpec(memory_space=pltpu.SMEM)


def matmul(left, right):
    return jnp.dot(left, right, preferred_element_type=f32)


def against_rows(left, right):
    return lax.dot_general(left, right, (((1,), (1,)), ((), ())), preferred_element_type=f32)


def limit(mebibytes):
    return pltpu.CompilerParams(vmem_limit_bytes=mebibytes * 1024 * 1024)


def cost(macs, nbytes):
    return pl.CostEstimate(flops=2 * macs, bytes_accessed=nbytes, transcendentals=0)


vmem = pl.BlockSpec(memory_space=pltpu.VMEM)
anywhere = pl.BlockSpec(memory_space=pl.ANY)


def shape(dims, dtype=bf16):
    return jax.ShapeDtypeStruct(dims, dtype)


def after(value, *earlier):
    return pl.pallas_call(
        lambda *refs: None,
        out_shape=shape(value.shape, value.dtype),
        in_specs=[anywhere] * (1 + len(earlier)),
        out_specs=anywhere,
        input_output_aliases={0: 0},
        compiler_params=limit(1),
    )(value, *earlier)


def share_kernel(value, out):
    rows = out.shape[0]
    place = lax.axis_index("rep") & 3
    out[...] = value[pl.ds(pl.multiple_of(place * rows, rows), rows)]


def share(value):
    return pl.pallas_call(
        share_kernel,
        out_shape=shape((value.shape[0] // 4, value.shape[1])),
        in_specs=[vmem],
        out_specs=vmem,
        compiler_params=limit(1),
        cost_estimate=cost(3 * 10**9, value.size),
    )(value)


def assemble_kernel(own, across, behind, upper, lower, out):
    rows = own.shape[0]
    half = rows // 2
    for place in range(4):

        @pl.when((lax.axis_index("rep") & 3) == place)
        def _():
            out[place * rows : (place + 1) * rows] = own[...]
            out[(place ^ 1) * rows : ((place ^ 1) + 1) * rows] = across[...]
            out[(place ^ 2) * rows : ((place ^ 2) + 1) * rows] = behind[...]
            out[(place ^ 3) * rows : (place ^ 3) * rows + half] = upper[...]
            out[(place ^ 3) * rows + half : ((place ^ 3) + 1) * rows] = lower[...]


def normalized(tokens):
    values = tokens.astype(f32)
    center = values - jnp.mean(values, axis=1, keepdims=True)
    spread = jnp.mean(center * center, axis=1, keepdims=True)
    return (center * lax.rsqrt(spread + 1e-05)).astype(bf16)


def gelu_both(values):
    coeff = math.sqrt(2.0 / math.pi)
    square = values * values
    gate = 0.5 + 0.5 * jnp.tanh(coeff * values * (1.0 + 0.044715 * square))
    hidden = values * gate
    slope = gate + hidden * (1.0 - gate) * (2.0 * coeff + 6.0 * 0.044715 * coeff * square)
    return hidden.astype(bf16), slope.astype(bf16)


def forward_core(tokens, weights_in, weights_out, normed_t, slopes, total, ready=None):
    count, width = tokens.shape
    block = weights_in[0].shape[1]
    tile = min(256, block)
    normed = normalized(tokens[...])
    normed_t[...] = normed.T
    for side in range(2):
        for at in range(0, block, tile):
            if ready is not None and side + at == 0:
                ready[0].wait()
            values = matmul(normed, weights_in[side][:, at : at + tile]) * (width**-0.5)
            hidden, slopes[side][:, at : at + tile] = gelu_both(values)
            if ready is not None and side + at == 0:
                ready[1].wait()
            term = matmul(hidden, weights_out[side][at : at + tile])
            if side + at == 0:
                total[...] = term
            else:
                total[...] += term


def forward_kernel(
    tokens_from, in_from, mate_in, out_from, mate_out, normed_t, slope, slope_mate, out, *scratch
):
    total, tokens, own_in, own_out, done = scratch
    copies = [
        pltpu.make_async_copy(source, target, done.at[at])
        for at, (source, target) in enumerate(
            ((tokens_from, tokens), (in_from, own_in), (out_from, own_out))
        )
    ]
    for copy in copies:
        copy.start()
    copies[0].wait()
    weights = (own_in, mate_in), (own_out, mate_out)
    forward_core(tokens, *weights, normed_t, (slope, slope_mate), total, copies[1:])
    out[...] = total[...].astype(bf16)


def forward_far_kernel(*refs):
    pieces = refs[:5]
    own_in, mate_in, own_out, mate_out, normed_t, slope, slope_mate = refs[5:12]
    out, total, tokens = refs[12:]
    assemble_kernel(*pieces, tokens)
    weights = (own_in, mate_in), (own_out, mate_out)
    forward_core(tokens, *weights, normed_t, (slope, slope_mate), total)
    count = tokens.shape[0]
    values = tokens[...].astype(f32)
    ahead = pltpu.roll(values, count - 1, 0)
    rank = lax.broadcasted_iota(jnp.int32, values.shape, 0)
    base = total[...] + values - ahead
    out[...] = jnp.where(rank == count - 1, 0.0, base)


def forward(given, count, weights, far):
    width, block = weights[0].shape
    outs = (
        shape((width, count)),
        shape((count, block)),
        shape((count, block)),
        shape((count, width), f32 if far else bf16),
    )
    scratch = [pltpu.VMEM((count, width), f32), pltpu.VMEM((count, width), bf16)]
    specs = [vmem] * (len(given) + len(weights))
    if not far:
        specs = [anywhere, anywhere, vmem, anywhere, vmem]
        scratch += [pltpu.VMEM(value.shape, bf16) for value in (weights[0], weights[2])]
        scratch.append(pltpu.SemaphoreType.DMA((3,)))
    return pl.pallas_call(
        forward_far_kernel if far else forward_kernel,
        out_shape=outs,
        in_specs=specs,
        out_specs=[vmem for out in outs],
        scratch_shapes=scratch,
        compiler_params=limit(20),
        cost_estimate=cost(4 * count * width * block, 8 * width * block),
    )(*given, *weights)


def errors_kernel(base, sent, *refs):
    errors = refs[-1]
    result = base[...] + sent[...].astype(f32)
    rank = lax.broadcasted_iota(jnp.int32, result.shape, 0)
    errors[...] = jnp.where(rank == result.shape[0] - 1, 0.0, result).astype(bf16)


def errors_of(base, sent, *earlier):
    return pl.pallas_call(
        errors_kernel,
        out_shape=shape(base.shape),
        in_specs=[vmem, vmem] + [anywhere] * len(earlier),
        out_specs=vmem,
        compiler_params=limit(8),
        cost_estimate=cost(0, 8 * base.size),
    )(base, sent, *earlier)


def hidden_kernel(errors, weight, slope, *refs):
    out = refs[-1]
    tile = min(256, weight.shape[0])
    for at in range(0, weight.shape[0], tile):
        cols = slice(at, at + tile)
        product = against_rows(errors[...], weight[cols]) * slope[:, cols].astype(f32)
        out[:, cols] = product.astype(bf16)


def hidden_of(errors, weight, slope, *earlier):
    count, width = errors.shape
    block = weight.shape[0]
    return pl.pallas_call(
        hidden_kernel,
        out_shape=shape((count, block)),
        in_specs=[vmem] * 3 + [anywhere] * len(earlier),
        out_specs=vmem,
        compiler_params=limit(8),
        cost_estimate=cost(count * width * block, 2 * width * block),
    )(errors, weight, slope, *earlier)


def update_kernel(start, heat, *refs):
    grads, normed = refs[:4], refs[4:8]
    params, noise = refs[8:10]
    out = refs[-1]
    here = slice(start, start + out.shape[0])
    total = 0.0
    for values, grad in zip(normed, grads):
        total += matmul(values[here], grad[...])
    current = params[0, here].astype(f32)
    strength = jnp.sqrt(jnp.full((1, out.shape[1]), 2.0 * drift_stride * heat[0], f32))
    slope = total * params.shape[1] ** -0.5
    moved = current - drift_stride * (slope + current) + strength * noise[0, here].astype(f32)
    out[...] = moved.astype(bf16)


def update(start, rows, heat, grads, normed, params, noise, *earlier):
    width, count = normed[0].shape
    block = grads[0].shape[1]
    return pl.pallas_call(
        functools.partial(update_kernel, start),
        out_shape=shape((rows, block)),
        in_specs=[smem] + [vmem] * 10 + [anywhere] * len(earlier),
        out_specs=vmem,
        compiler_params=limit(4),
        cost_estimate=cost(4 * rows * count * block, 8 * rows * count),
    )(heat, *grads, *normed, params, noise, *earlier)


def role(mate, swapped):
    rank = lax.axis_index("rep")
    odd = rank & 1
    taken = swapped[0] == 1
    return odd, taken & (mate[0] == rank + 1 - 2 * odd), taken & (mate[0] == rank - 1 + 2 * odd)


def finish_kernel(start, stop, count, mate, swapped, *refs):
    own, across, beyond = (refs[i * count : (i + 1) * count] for i in range(3))
    result, gaps, out, done = refs[-4:]
    odd, near_taken, far_taken = role(mate, swapped)
    near_sum = far_sum = 0.0
    at = 0
    for part in range(count):
        mine, near, far = (pieces[part][...] for pieces in (own, across, beyond))
        out[at : at + mine.shape[0]] = jnp.where(near_taken, near, jnp.where(far_taken, far, mine))
        at += mine.shape[0]
        mine = mine.astype(f32)
        near = near.astype(f32) - mine
        far = far.astype(f32) - mine
        near_sum += jnp.sum(near * near, axis=0, keepdims=True)
        far_sum += jnp.sum(far * far, axis=0, keepdims=True)
    copy = pltpu.make_async_copy(out, result.at[0, pl.ds(start, stop - start)], done)
    copy.start()
    if start > 0:
        so_far = refs[3 * count]
        near_sum += so_far[0, 0:1]
        far_sum += so_far[0, 1:2]
    if stop == result.shape[1]:
        near_sum *= 1.0 / result.shape[1]
        far_sum *= 1.0 / result.shape[1]
        near_sum, far_sum = (
            jnp.where(odd == 1, near_sum, far_sum),
            jnp.where(odd == 1, far_sum, near_sum),
        )
    gaps[0, 0:1] = near_sum
    gaps[0, 1:2] = far_sum
    copy.wait()


def finish(width, start, pairing, own, across, beyond, so_far):
    count = len(own)
    block = own[0].shape[1]
    stop = start + sum(value.shape[0] for value in own)
    given = [*own, *across, *beyond]
    specs = [vmem] * len(given)
    aliases = {}
    if start > 0:
        given += [so_far[1], so_far[0]]
        specs += [vmem, anywhere]
        aliases = {1 + len(given): 0}
    return pl.pallas_call(
        functools.partial(finish_kernel, start, stop, count),
        out_shape=(shape((1, width, block)), shape((1, 2, block), f32)),
        in_specs=[smem, smem] + specs,
        out_specs=(anywhere, vmem),
        scratch_shapes=[pltpu.VMEM((stop - start, block), bf16), pltpu.SemaphoreType.DMA],
        input_output_aliases=aliases,
        compiler_params=limit(4),
        cost_estimate=cost(0, 8 * (stop - start) * block),
    )(*pairing, *given)


def body(
    residual_flow,
    rooted_input_matrix,
    chain_normal_draws,
    output_matrix,
    chain_heat,
    matched_chain,
    swap_mask,
):
    replicas = lax.axis_size("rep")
    params = rooted_input_matrix[0]
    block = params.shape[1]
    count = residual_flow.shape[0]

    def to_core(value):
        return lax.ppermute(value, "dp", [(i, i ^ 1) for i in range(4)])

    def to_chip(value):
        return lax.ppermute(value, "dp", [(i, i ^ 2) for i in range(4)])

    def to_mate(value):
        return lax.ppermute(value, "rep", [(i, i ^ 1) for i in range(replicas)])

    def to_pair(value):
        return lax.ppermute(value, "rep", [(i, i ^ 2) for i in range(replicas)])

    def to_next(value):
        pairs = [(i, (i + (2 if i % 2 == 0 else -2)) % replicas) for i in range(replicas)]
        return lax.ppermute(value, "rep", pairs)

    def step_one(own):
        return to_mate(own), to_pair(own)

    def step_two(own, across, behind):
        half = own.shape[0] // 2
        return own, across, behind, to_mate(behind[:half]), to_pair(across[half:])

    mate_in = to_core(params)
    mate_out = to_core(output_matrix)
    token_own = to_chip(share(residual_flow))
    weights = (params, mate_in, output_matrix, mate_out)
    normed, slope, slope_send, part = forward((residual_flow,), count, weights, False)
    sent = to_chip(after(part, token_own))
    token_own = after(token_own, part)
    token_across, token_behind = step_one(token_own)
    token_pieces = step_two(token_own, token_across, token_behind)
    normed_mate = to_core(normed)
    slope_mate = to_core(slope_send)
    far, far_slope, far_slope_send, base = forward(token_pieces, count, weights, True)
    far_mate = to_core(far)
    far_slope_mate = to_core(far_slope_send)

    errors = errors_of(base, sent, normed_mate, slope_mate)
    back = to_chip(errors)
    far_grads = [
        hidden_of(errors, output_matrix, far_slope),
        hidden_of(to_core(errors), output_matrix, far_slope_mate),
    ]
    back = after(back, *far_grads, far_mate)
    near_grads = [
        hidden_of(back, output_matrix, slope),
        hidden_of(to_core(back), output_matrix, slope_mate),
    ]
    grads = near_grads + far_grads

    pairing = (matched_chain, swap_mask)
    width = params.shape[0]
    sizes = [width * part // 8 for part in (1, 2, 2, 2, 1)]
    starts = [sum(sizes[:chunk]) for chunk in range(len(sizes))]
    own, across, beyond = [], [], []
    for chunk, (start, rows) in enumerate(zip(starts, sizes)):
        fresh = update(
            start,
            rows,
            chain_heat,
            grads,
            (normed, normed_mate, far, far_mate),
            rooted_input_matrix,
            chain_normal_draws,
            *own[-1:],
        )
        if chunk >= 2:
            fresh = after(fresh, across[chunk - 2])
        own.append(fresh)
        across.append(to_mate(fresh))
    done = None
    cut = len(sizes) - 1
    for first, stop in ((0, cut), (cut, cut + 1)):
        for chunk in range(first, stop):
            if chunk >= 2:
                across[chunk] = after(across[chunk], beyond[chunk - 2])
            beyond.append(to_next(across[chunk]))
        given = (pieces[first:stop] for pieces in (own, across, beyond))
        done = finish(width, starts[first], pairing, *given, done)
    return done


def solution(mesh):
    placed = (
        P("dp", None),
        P("rep", None, "dp"),
        P("rep", None, "dp"),
        P("dp", None),
        P("rep"),
        P("rep"),
        P("rep"),
    )
    return jax.shard_map(
        body,
        mesh=mesh,
        in_specs=placed,
        out_specs=(P("rep", None, "dp"), P("rep", None, "dp")),
        check_vma=False,
    )
```

```python
import functools
import math

import jax
import jax.numpy as jnp
from jax import lax
from jax.experimental import pallas as pl
from jax.experimental.pallas import tpu as pltpu
from jax.sharding import PartitionSpec as P

drift_stride = 0.5
f32 = jnp.float32
bf16 = jnp.bfloat16
smem = pl.BlockSpec(memory_space=pltpu.SMEM)


def matmul(left, right):
    return jnp.dot(left, right, preferred_element_type=f32)


def against_rows(left, right):
    return lax.dot_general(left, right, (((1,), (1,)), ((), ())), preferred_element_type=f32)


def limit(mebibytes):
    return pltpu.CompilerParams(vmem_limit_bytes=mebibytes * 1024 * 1024)


def cost(macs, nbytes):
    return pl.CostEstimate(flops=2 * macs, bytes_accessed=nbytes, transcendentals=0)


vmem = pl.BlockSpec(memory_space=pltpu.VMEM)
anywhere = pl.BlockSpec(memory_space=pl.ANY)


def shape(dims, dtype=bf16):
    return jax.ShapeDtypeStruct(dims, dtype)


def after(value, *earlier):
    return pl.pallas_call(
        lambda *refs: None,
        out_shape=shape(value.shape, value.dtype),
        in_specs=[anywhere] * (1 + len(earlier)),
        out_specs=anywhere,
        input_output_aliases={0: 0},
        compiler_params=limit(1),
    )(value, *earlier)


def share_kernel(value, out, done):
    rows = out.shape[0]
    place = lax.axis_index("rep") & 3
    here = pl.ds(pl.multiple_of(place * rows, rows), rows)
    copy = pltpu.make_async_copy(value.at[here], out, done)
    copy.start()
    copy.wait()


def share(value):
    return pl.pallas_call(
        share_kernel,
        out_shape=shape((value.shape[0] // 4, value.shape[1])),
        in_specs=[anywhere],
        out_specs=vmem,
        scratch_shapes=[pltpu.SemaphoreType.DMA],
        compiler_params=limit(1),
        cost_estimate=cost(3 * 10**9, value.size),
    )(value)


def assemble_kernel(own, across, behind, upper, lower, out):
    rows = own.shape[0]
    half = rows // 2
    for place in range(4):

        @pl.when((lax.axis_index("rep") & 3) == place)
        def _():
            out[place * rows : (place + 1) * rows] = own[...]
            out[(place ^ 1) * rows : ((place ^ 1) + 1) * rows] = across[...]
            out[(place ^ 2) * rows : ((place ^ 2) + 1) * rows] = behind[...]
            out[(place ^ 3) * rows : (place ^ 3) * rows + half] = upper[...]
            out[(place ^ 3) * rows + half : ((place ^ 3) + 1) * rows] = lower[...]


def normalized(tokens):
    values = tokens.astype(f32)
    center = values - jnp.mean(values, axis=1, keepdims=True)
    spread = jnp.mean(center * center, axis=1, keepdims=True)
    return (center * lax.rsqrt(spread + 1e-05)).astype(bf16)


def gelu_both(values):
    coeff = math.sqrt(2.0 / math.pi)
    square = values * values
    gate = 0.5 + 0.5 * jnp.tanh(coeff * values * (1.0 + 0.044715 * square))
    hidden = values * gate
    slope = gate + hidden * (1.0 - gate) * (2.0 * coeff + 6.0 * 0.044715 * coeff * square)
    return hidden.astype(bf16), slope.astype(bf16)


def forward_core(tokens, weights_in, weights_out, normed_t, slopes, part, base, total):
    count, width = tokens.shape
    block = weights_in[0].shape[1]
    tile = min(256, block)
    normed = normalized(tokens[...])
    normed_t[...] = normed.T
    for side in range(2):
        for at in range(0, block, tile):
            values = matmul(normed, weights_in[side][:, at : at + tile]) * (width**-0.5)
            hidden, slopes[side][:, at : at + tile] = gelu_both(values)
            term = matmul(hidden, weights_out[side][at : at + tile])
            if side + at == 0:
                total[...] = term
            else:
                total[...] += term
    part[...] = total[...].astype(bf16)
    values = tokens[...].astype(f32)
    ahead = pltpu.roll(values, count - 1, 0)
    rank = lax.broadcasted_iota(jnp.int32, values.shape, 0)
    base[...] = jnp.where(rank == count - 1, 0.0, total[...] + values - ahead)


def forward_kernel(pieces, skipped, *refs):
    given = refs[:pieces]
    own_in, mate_in, own_out, mate_out = refs[pieces : pieces + 4]
    normed_t, slope, slope_mate, part, base, total, tokens = refs[pieces + 4 + skipped :]
    if pieces > 1:
        assemble_kernel(*given, tokens)
    else:
        tokens = given[0]
    weights = (own_in, mate_in), (own_out, mate_out)
    forward_core(tokens, *weights, normed_t, (slope, slope_mate), part, base, total)


def forward(given, count, weights, *earlier):
    width, block = weights[0].shape
    outs = (
        shape((width, count)),
        shape((count, block)),
        shape((count, block)),
        shape((count, width)),
        shape((count, width), f32),
    )
    return pl.pallas_call(
        functools.partial(forward_kernel, len(given), len(earlier)),
        out_shape=outs,
        in_specs=[vmem] * (len(given) + len(weights)) + [anywhere] * len(earlier),
        out_specs=[vmem for out in outs],
        scratch_shapes=[pltpu.VMEM((count, width), f32), pltpu.VMEM((count, width), bf16)],
        compiler_params=limit(12),
        cost_estimate=cost(4 * count * width * block, 8 * width * block),
    )(*given, *weights, *earlier)


def errors_kernel(base, sent, *refs):
    errors = refs[-1]
    result = base[...] + sent[...].astype(f32)
    rank = lax.broadcasted_iota(jnp.int32, result.shape, 0)
    errors[...] = jnp.where(rank == result.shape[0] - 1, 0.0, result).astype(bf16)


def errors_of(base, sent, *earlier):
    return pl.pallas_call(
        errors_kernel,
        out_shape=shape(base.shape),
        in_specs=[vmem, vmem] + [anywhere] * len(earlier),
        out_specs=vmem,
        compiler_params=limit(2),
        cost_estimate=cost(0, 8 * base.size),
    )(base, sent, *earlier)


def strength_kernel(heat, out):
    out[...] = jnp.sqrt(jnp.full(out.shape, 2.0 * drift_stride * heat[0], f32))


def strength_of(heat, block):
    return pl.pallas_call(
        strength_kernel,
        out_shape=shape((1, block), f32),
        in_specs=[smem],
        out_specs=vmem,
        compiler_params=limit(1),
        cost_estimate=cost(0, 4 * block),
    )(heat)


def hidden_kernel(errors, weight, slope, *refs):
    out = refs[-1]
    tile = min(256, weight.shape[0])
    for at in range(0, weight.shape[0], tile):
        cols = slice(at, at + tile)
        product = against_rows(errors[...], weight[cols]) * slope[:, cols].astype(f32)
        out[:, cols] = product.astype(bf16)


def hidden_of(errors, weight, slope, *earlier):
    count, width = errors.shape
    block = weight.shape[0]
    return pl.pallas_call(
        hidden_kernel,
        out_shape=shape((count, block)),
        in_specs=[vmem] * 3 + [anywhere] * len(earlier),
        out_specs=vmem,
        compiler_params=limit(8),
        cost_estimate=cost(count * width * block, 2 * width * block),
    )(errors, weight, slope, *earlier)


def update_kernel(start, strength, *refs):
    grads, normed = refs[:4], refs[4:8]
    params, noise = refs[8:10]
    out = refs[-1]
    here = slice(start, start + out.shape[0])
    total = 0.0
    for values, grad in zip(normed, grads):
        total += matmul(values[here], grad[...])
    current = params[0, here].astype(f32)
    slope = total * params.shape[1] ** -0.5
    moved = current - drift_stride * (slope + current) + strength[...] * noise[0, here].astype(f32)
    out[...] = moved.astype(bf16)


def update(start, rows, heat, grads, normed, params, noise, *earlier):
    width, count = normed[0].shape
    block = grads[0].shape[1]
    return pl.pallas_call(
        functools.partial(update_kernel, start),
        out_shape=shape((rows, block)),
        in_specs=[vmem] * 11 + [anywhere] * len(earlier),
        out_specs=vmem,
        compiler_params=limit(4),
        cost_estimate=cost(4 * rows * count * block, 8 * rows * count),
    )(heat, *grads, *normed, params, noise, *earlier)


def role(mate, swapped):
    rank = lax.axis_index("rep")
    odd = rank & 1
    taken = swapped[0] == 1
    return odd, taken & (mate[0] == rank + 1 - 2 * odd), taken & (mate[0] == rank - 1 + 2 * odd)


def finish_kernel(start, stop, count, mate, swapped, *refs):
    own, across, beyond = (refs[i * count : (i + 1) * count] for i in range(3))
    result, gaps, out, done = refs[-4:]
    odd, near_taken, far_taken = role(mate, swapped)
    at = 0
    for mine, near, far in zip(own, across, beyond):
        out[at : at + mine.shape[0]] = jnp.where(
            near_taken, near[...], jnp.where(far_taken, far[...], mine[...])
        )
        at += mine.shape[0]
    copy = pltpu.make_async_copy(out, result.at[0, pl.ds(start, stop - start)], done)
    copy.start()
    near_sum = far_sum = 0.0
    for part in range(count):
        mine, near, far = (pieces[part][...].astype(f32) for pieces in (own, across, beyond))
        near_sum += jnp.sum((near - mine) * (near - mine), axis=0, keepdims=True)
        far_sum += jnp.sum((far - mine) * (far - mine), axis=0, keepdims=True)
    if start > 0:
        so_far = refs[3 * count]
        near_sum += so_far[0, 0:1]
        far_sum += so_far[0, 1:2]
    if stop == result.shape[1]:
        near_sum *= 1.0 / result.shape[1]
        far_sum *= 1.0 / result.shape[1]
        near_sum, far_sum = (
            jnp.where(odd == 1, near_sum, far_sum),
            jnp.where(odd == 1, far_sum, near_sum),
        )
    gaps[0, 0:1] = near_sum
    gaps[0, 1:2] = far_sum
    copy.wait()


def finish(width, start, pairing, own, across, beyond, so_far):
    count = len(own)
    block = own[0].shape[1]
    stop = start + sum(value.shape[0] for value in own)
    given = [*own, *across, *beyond]
    specs = [vmem] * len(given)
    aliases = {}
    if start > 0:
        given += [so_far[1], so_far[0]]
        specs += [vmem, anywhere]
        aliases = {1 + len(given): 0}
    return pl.pallas_call(
        functools.partial(finish_kernel, start, stop, count),
        out_shape=(shape((1, width, block)), shape((1, 2, block), f32)),
        in_specs=[smem, smem] + specs,
        out_specs=(anywhere, vmem),
        scratch_shapes=[pltpu.VMEM((stop - start, block), bf16), pltpu.SemaphoreType.DMA],
        input_output_aliases=aliases,
        compiler_params=limit(4),
        cost_estimate=cost(0, 8 * (stop - start) * block),
    )(*pairing, *given)


def body(
    residual_flow,
    rooted_input_matrix,
    chain_normal_draws,
    output_matrix,
    chain_heat,
    matched_chain,
    swap_mask,
):
    replicas = lax.axis_size("rep")
    params = rooted_input_matrix[0]
    block = params.shape[1]
    count = residual_flow.shape[0]

    def to_core(value):
        return lax.ppermute(value, "dp", [(i, i ^ 1) for i in range(4)])

    def to_chip(value):
        return lax.ppermute(value, "dp", [(i, i ^ 2) for i in range(4)])

    def to_mate(value):
        return lax.ppermute(value, "rep", [(i, i ^ 1) for i in range(replicas)])

    def to_pair(value):
        return lax.ppermute(value, "rep", [(i, i ^ 2) for i in range(replicas)])

    def to_next(value):
        pairs = [(i, (i + (2 if i % 2 == 0 else -2)) % replicas) for i in range(replicas)]
        return lax.ppermute(value, "rep", pairs)

    def step_one(own):
        return to_mate(own), to_pair(own)

    def step_two(own, across, behind):
        half = own.shape[0] // 2
        return own, across, behind, to_mate(behind[:half]), to_pair(across[half:])

    mate_in = to_core(params)
    mate_out = to_core(output_matrix)
    token_share = share(residual_flow)
    token_own = to_chip(token_share)
    weights = (params, mate_in, output_matrix, mate_out)
    normed, slope, slope_send, part, base = forward((residual_flow,), count, weights)
    sent = to_chip(after(part, token_own))
    token_own = after(token_own, part)
    token_across, token_behind = step_one(token_own)
    token_pieces = step_two(token_own, token_across, token_behind)
    normed_mate = to_core(normed)
    slope_mate = to_core(slope_send)
    far, far_slope, far_slope_send, far_part, far_base = forward(token_pieces, count, weights)
    far_sent = to_chip(far_part)
    far_mate = to_core(far)
    far_slope_mate = to_core(far_slope_send)

    strength = strength_of(chain_heat, block)
    errors = errors_of(far_base, sent, normed_mate, slope_mate, strength)
    far_grads = [
        hidden_of(errors, output_matrix, far_slope),
        hidden_of(to_core(errors), output_matrix, far_slope_mate),
    ]
    errors = errors_of(base, far_sent, *far_grads, far_mate)
    near_grads = [
        hidden_of(errors, output_matrix, slope),
        hidden_of(to_core(errors), output_matrix, slope_mate),
    ]
    grads = near_grads + far_grads

    pairing = (matched_chain, swap_mask)
    width = params.shape[0]
    sizes = [width * part // 8 for part in (2, 2, 2, 2)]
    starts = [sum(sizes[:chunk]) for chunk in range(len(sizes))]
    own, across, beyond = [], [], []
    for chunk, (start, rows) in enumerate(zip(starts, sizes)):
        fresh = update(
            start,
            rows,
            strength,
            grads,
            (normed, normed_mate, far, far_mate),
            rooted_input_matrix,
            chain_normal_draws,
            *own[-1:],
        )
        own.append(fresh)
        across.append(to_mate(fresh))
    done = None
    cut = len(sizes) - 1
    for first, stop in ((0, cut), (cut, cut + 1)):
        for chunk in range(first, stop):
            if chunk >= 2:
                across[chunk] = after(across[chunk], beyond[chunk - 2])
            beyond.append(to_next(across[chunk]))
        given = (pieces[first:stop] for pieces in (own, across, beyond))
        done = finish(width, starts[first], pairing, *given, done)
    return done


def solution(mesh):
    placed = (
        P("dp", None),
        P("rep", None, "dp"),
        P("rep", None, "dp"),
        P("dp", None),
        P("rep"),
        P("rep"),
        P("rep"),
    )
    return jax.shard_map(
        body,
        mesh=mesh,
        in_specs=placed,
        out_specs=(P("rep", None, "dp"), P("rep", None, "dp")),
        check_vma=False,
    )
```

```python
import functools
import math

import jax
import jax.numpy as jnp
from jax import lax
from jax.experimental import pallas as pl
from jax.experimental.pallas import tpu as pltpu
from jax.sharding import PartitionSpec as P

drift_stride = 0.5
f32 = jnp.float32
bf16 = jnp.bfloat16
smem = pl.BlockSpec(memory_space=pltpu.SMEM)


def matmul(left, right):
    return jnp.dot(left, right, preferred_element_type=f32)


def against_rows(left, right):
    return lax.dot_general(left, right, (((1,), (1,)), ((), ())), preferred_element_type=f32)


def limit(mebibytes):
    return pltpu.CompilerParams(vmem_limit_bytes=mebibytes * 1024 * 1024)


def cost(macs, nbytes):
    return pl.CostEstimate(flops=2 * macs, bytes_accessed=nbytes, transcendentals=0)


vmem = pl.BlockSpec(memory_space=pltpu.VMEM)
anywhere = pl.BlockSpec(memory_space=pl.ANY)


def shape(dims, dtype=bf16):
    return jax.ShapeDtypeStruct(dims, dtype)


def after(value, *earlier):
    return pl.pallas_call(
        lambda *refs: None,
        out_shape=shape(value.shape, value.dtype),
        in_specs=[anywhere] * (1 + len(earlier)),
        out_specs=anywhere,
        input_output_aliases={0: 0},
        compiler_params=limit(1),
    )(value, *earlier)


def share_kernel(value, out, done):
    rows = out.shape[0]
    place = lax.axis_index("rep") & 3
    here = pl.ds(pl.multiple_of(place * rows, rows), rows)
    copy = pltpu.make_async_copy(value.at[here], out, done)
    copy.start()
    copy.wait()


def share(value):
    return pl.pallas_call(
        share_kernel,
        out_shape=shape((value.shape[0] // 4, value.shape[1])),
        in_specs=[anywhere],
        out_specs=vmem,
        scratch_shapes=[pltpu.SemaphoreType.DMA],
        compiler_params=limit(1),
        cost_estimate=cost(3 * 10**9, value.size),
    )(value)


def assemble_kernel(own, across, behind, upper, lower, out):
    rows = own.shape[0]
    half = rows // 2
    for place in range(4):

        @pl.when((lax.axis_index("rep") & 3) == place)
        def _():
            out[place * rows : (place + 1) * rows] = own[...]
            out[(place ^ 1) * rows : ((place ^ 1) + 1) * rows] = across[...]
            out[(place ^ 2) * rows : ((place ^ 2) + 1) * rows] = behind[...]
            out[(place ^ 3) * rows : (place ^ 3) * rows + half] = upper[...]
            out[(place ^ 3) * rows + half : ((place ^ 3) + 1) * rows] = lower[...]


def normalized(tokens):
    values = tokens.astype(f32)
    center = values - jnp.mean(values, axis=1, keepdims=True)
    spread = jnp.mean(center * center, axis=1, keepdims=True)
    return (center * lax.rsqrt(spread + 1e-05)).astype(bf16)


def gelu_both(values):
    coeff = math.sqrt(2.0 / math.pi)
    square = values * values
    gate = 0.5 + 0.5 * jnp.tanh(coeff * values * (1.0 + 0.044715 * square))
    hidden = values * gate
    slope = gate + hidden * (1.0 - gate) * (2.0 * coeff + 6.0 * 0.044715 * coeff * square)
    return hidden.astype(bf16), slope.astype(bf16)


def forward_core(tokens, weights_in, weights_out, normed_t, slopes, part, base, total):
    count, width = tokens.shape
    block = weights_in[0].shape[1]
    tile = min(256, block)
    normed = normalized(tokens[...])
    normed_t[...] = normed.T
    for side in range(2):
        for at in range(0, block, tile):
            values = matmul(normed, weights_in[side][:, at : at + tile]) * (width**-0.5)
            hidden, slopes[side][:, at : at + tile] = gelu_both(values)
            term = matmul(hidden, weights_out[side][at : at + tile])
            if side + at == 0:
                total[...] = term
            else:
                total[...] += term
    part[...] = total[...].astype(bf16)
    values = tokens[...].astype(f32)
    ahead = pltpu.roll(values, count - 1, 0)
    rank = lax.broadcasted_iota(jnp.int32, values.shape, 0)
    base[...] = jnp.where(rank == count - 1, 0.0, total[...] + values - ahead)


def forward_kernel(pieces, skipped, *refs):
    given = refs[:pieces]
    own_in, mate_in, own_out, mate_out = refs[pieces : pieces + 4]
    normed_t, slope, slope_mate, part, base, total, tokens = refs[pieces + 4 + skipped :]
    if pieces > 1:
        assemble_kernel(*given, tokens)
    else:
        tokens = given[0]
    weights = (own_in, mate_in), (own_out, mate_out)
    forward_core(tokens, *weights, normed_t, (slope, slope_mate), part, base, total)


def forward(given, count, weights, *earlier):
    width, block = weights[0].shape
    outs = (
        shape((width, count)),
        shape((count, block)),
        shape((count, block)),
        shape((count, width)),
        shape((count, width), f32),
    )
    return pl.pallas_call(
        functools.partial(forward_kernel, len(given), len(earlier)),
        out_shape=outs,
        in_specs=[vmem] * (len(given) + len(weights)) + [anywhere] * len(earlier),
        out_specs=[vmem for out in outs],
        scratch_shapes=[pltpu.VMEM((count, width), f32), pltpu.VMEM((count, width), bf16)],
        compiler_params=limit(12),
        cost_estimate=cost(0, 1000),
    )(*given, *weights, *earlier)


def errors_kernel(base, sent, *refs):
    errors = refs[-1]
    result = base[...] + sent[...].astype(f32)
    rank = lax.broadcasted_iota(jnp.int32, result.shape, 0)
    errors[...] = jnp.where(rank == result.shape[0] - 1, 0.0, result).astype(bf16)


def errors_of(base, sent, *earlier):
    return pl.pallas_call(
        errors_kernel,
        out_shape=shape(base.shape),
        in_specs=[vmem, vmem] + [anywhere] * len(earlier),
        out_specs=vmem,
        compiler_params=limit(2),
        cost_estimate=cost(0, 8 * base.size),
    )(base, sent, *earlier)


def strength_kernel(heat, out):
    out[...] = jnp.sqrt(jnp.full(out.shape, 2.0 * drift_stride * heat[0], f32))


def strength_of(heat, block):
    return pl.pallas_call(
        strength_kernel,
        out_shape=shape((1, block), f32),
        in_specs=[smem],
        out_specs=vmem,
        compiler_params=limit(1),
        cost_estimate=cost(0, 4 * block),
    )(heat)


def hidden_kernel(errors, weight, slope, *refs):
    out = refs[-1]
    tile = min(256, weight.shape[0])
    for at in range(0, weight.shape[0], tile):
        cols = slice(at, at + tile)
        product = against_rows(errors[...], weight[cols]) * slope[:, cols].astype(f32)
        out[:, cols] = product.astype(bf16)


def hidden_of(errors, weight, slope, *earlier):
    count, width = errors.shape
    block = weight.shape[0]
    return pl.pallas_call(
        hidden_kernel,
        out_shape=shape((count, block)),
        in_specs=[vmem] * 3 + [anywhere] * len(earlier),
        out_specs=vmem,
        compiler_params=limit(8),
        cost_estimate=cost(count * width * block, 2 * width * block),
    )(errors, weight, slope, *earlier)


def begin_kernel(strength, first, second, normed, normed_mate, params, noise, out):
    width = params.shape[1]
    rows = width // 4
    for start in range(0, width, rows):
        here = slice(start, start + rows)
        slope = matmul(normed[here], first[...]) + matmul(normed_mate[here], second[...])
        out[here] = (
            (1.0 - drift_stride) * params[0, here].astype(f32)
            + strength[...] * noise[0, here].astype(f32)
            - (drift_stride * width**-0.5) * slope
        )


def begin(strength, grads, normed, params, noise):
    width, count = normed[0].shape
    block = grads[0].shape[1]
    return pl.pallas_call(
        begin_kernel,
        out_shape=shape((width, block), f32),
        in_specs=[vmem] * 7,
        out_specs=vmem,
        compiler_params=limit(4),
        cost_estimate=cost(2 * width * count * block, 8 * width * count),
    )(strength, *grads, *normed, params, noise)


def update_kernel(start, begun, first, second, normed, normed_mate, *rest):
    out = rest[-1]
    here = slice(start, start + out.shape[0])
    slope = matmul(normed[here], first[...]) + matmul(normed_mate[here], second[...])
    out[...] = (begun[here] - (drift_stride * normed.shape[0] ** -0.5) * slope).astype(bf16)


def update(start, rows, begun, grads, normed, *earlier):
    count = normed[0].shape[1]
    block = grads[0].shape[1]
    return pl.pallas_call(
        functools.partial(update_kernel, start),
        out_shape=shape((rows, block)),
        in_specs=[vmem] * 5 + [anywhere] * len(earlier),
        out_specs=vmem,
        compiler_params=limit(4),
        cost_estimate=cost(2 * rows * count * block, 8 * rows * count),
    )(begun, *grads, *normed, *earlier)


def role(mate, swapped):
    rank = lax.axis_index("rep")
    odd = rank & 1
    taken = swapped[0] == 1
    return odd, taken & (mate[0] == rank + 1 - 2 * odd), taken & (mate[0] == rank - 1 + 2 * odd)


def finish_kernel(start, stop, count, mate, swapped, *refs):
    own, across, beyond = (refs[i * count : (i + 1) * count] for i in range(3))
    result, gaps, out, done = refs[-4:]
    odd, near_taken, far_taken = role(mate, swapped)
    at = 0
    for mine, near, far in zip(own, across, beyond):
        out[at : at + mine.shape[0]] = jnp.where(
            near_taken, near[...], jnp.where(far_taken, far[...], mine[...])
        )
        at += mine.shape[0]
    copy = pltpu.make_async_copy(out, result.at[0, pl.ds(start, stop - start)], done)
    copy.start()
    near_sum = far_sum = 0.0
    for part in range(count):
        mine, near, far = (pieces[part][...].astype(f32) for pieces in (own, across, beyond))
        near_sum += jnp.sum((near - mine) * (near - mine), axis=0, keepdims=True)
        far_sum += jnp.sum((far - mine) * (far - mine), axis=0, keepdims=True)
    if start > 0:
        so_far = refs[3 * count]
        near_sum += so_far[0, 0:1]
        far_sum += so_far[0, 1:2]
    if stop == result.shape[1]:
        near_sum *= 1.0 / result.shape[1]
        far_sum *= 1.0 / result.shape[1]
        near_sum, far_sum = (
            jnp.where(odd == 1, near_sum, far_sum),
            jnp.where(odd == 1, far_sum, near_sum),
        )
    gaps[0, 0:1] = near_sum
    gaps[0, 1:2] = far_sum
    copy.wait()


def finish(width, start, pairing, own, across, beyond, so_far):
    count = len(own)
    block = own[0].shape[1]
    stop = start + sum(value.shape[0] for value in own)
    given = [*own, *across, *beyond]
    specs = [vmem] * len(given)
    aliases = {}
    if start > 0:
        given += [so_far[1], so_far[0]]
        specs += [vmem, anywhere]
        aliases = {1 + len(given): 0}
    return pl.pallas_call(
        functools.partial(finish_kernel, start, stop, count),
        out_shape=(shape((1, width, block)), shape((1, 2, block), f32)),
        in_specs=[smem, smem] + specs,
        out_specs=(anywhere, vmem),
        scratch_shapes=[pltpu.VMEM((stop - start, block), bf16), pltpu.SemaphoreType.DMA],
        input_output_aliases=aliases,
        compiler_params=limit(4),
        cost_estimate=cost(0, 8 * (stop - start) * block),
    )(*pairing, *given)


def body(
    residual_flow,
    rooted_input_matrix,
    chain_normal_draws,
    output_matrix,
    chain_heat,
    matched_chain,
    swap_mask,
):
    replicas = lax.axis_size("rep")
    params = rooted_input_matrix[0]
    block = params.shape[1]
    count = residual_flow.shape[0]

    def to_core(value):
        return lax.ppermute(value, "dp", [(i, i ^ 1) for i in range(4)])

    def to_chip(value):
        return lax.ppermute(value, "dp", [(i, i ^ 2) for i in range(4)])

    def to_mate(value):
        return lax.ppermute(value, "rep", [(i, i ^ 1) for i in range(replicas)])

    def to_pair(value):
        return lax.ppermute(value, "rep", [(i, i ^ 2) for i in range(replicas)])

    def to_next(value):
        pairs = [(i, (i + (2 if i % 2 == 0 else -2)) % replicas) for i in range(replicas)]
        return lax.ppermute(value, "rep", pairs)

    def step_one(own):
        return to_mate(own), to_pair(own)

    def step_two(own, across, behind):
        half = own.shape[0] // 2
        return own, across, behind, to_mate(behind[:half]), to_pair(across[half:])

    mate_in = to_core(params)
    mate_out = to_core(output_matrix)
    token_share = share(residual_flow)
    token_own = to_chip(token_share)
    weights = (params, mate_in, output_matrix, mate_out)
    normed, slope, slope_send, part, base = forward((residual_flow,), count, weights)
    sent = to_chip(after(part, token_own))
    token_own = after(token_own, part)
    token_across, token_behind = step_one(token_own)
    token_pieces = step_two(token_own, token_across, token_behind)
    normed_mate = to_core(normed)
    far, far_slope, far_slope_send, far_part, far_base = forward(token_pieces, count, weights)
    far_sent = to_chip(far_part)
    far_mate = to_core(far)

    strength = strength_of(chain_heat, block)
    errors = errors_of(far_base, sent, normed_mate, strength)
    far_grads = [
        hidden_of(errors, output_matrix, far_slope),
        to_core(hidden_of(errors, mate_out, far_slope_send)),
    ]
    begun = begin(
        strength, far_grads, (far, far_mate), rooted_input_matrix, chain_normal_draws
    )
    errors = errors_of(base, far_sent, begun)
    grads = [
        hidden_of(errors, output_matrix, slope),
        to_core(hidden_of(errors, mate_out, slope_send)),
    ]

    pairing = (matched_chain, swap_mask)
    width = params.shape[0]
    sizes = [width * part // 8 for part in (2, 2, 2, 2)]
    starts = [sum(sizes[:chunk]) for chunk in range(len(sizes))]
    own, across, beyond = [], [], []
    for chunk, (start, rows) in enumerate(zip(starts, sizes)):
        fresh = update(start, rows, begun, grads, (normed, normed_mate), *own[-1:])
        own.append(fresh)
        across.append(to_mate(fresh))
    done = None
    cut = len(sizes) - 1
    for first, stop in ((0, cut), (cut, cut + 1)):
        for chunk in range(first, stop):
            if chunk >= 2:
                across[chunk] = after(across[chunk], beyond[chunk - 2])
            beyond.append(to_next(across[chunk]))
        given = (pieces[first:stop] for pieces in (own, across, beyond))
        done = finish(width, starts[first], pairing, *given, done)
    return done


def solution(mesh):
    placed = (
        P("dp", None),
        P("rep", None, "dp"),
        P("rep", None, "dp"),
        P("dp", None),
        P("rep"),
        P("rep"),
        P("rep"),
    )
    return jax.shard_map(
        body,
        mesh=mesh,
        in_specs=placed,
        out_specs=(P("rep", None, "dp"), P("rep", None, "dp")),
        check_vma=False,
    )
```

```python
import functools
import math

import jax
import jax.numpy as jnp
from jax import lax
from jax.experimental import pallas as pl
from jax.experimental.pallas import tpu as pltpu
from jax.sharding import PartitionSpec as P

drift_stride = 0.5
f32 = jnp.float32
bf16 = jnp.bfloat16
smem = pl.BlockSpec(memory_space=pltpu.SMEM)


def matmul(left, right):
    return jnp.dot(left, right, preferred_element_type=f32)


def against_rows(left, right):
    return lax.dot_general(left, right, (((1,), (1,)), ((), ())), preferred_element_type=f32)


def limit(mebibytes):
    return pltpu.CompilerParams(vmem_limit_bytes=mebibytes * 1024 * 1024)


def cost(macs, nbytes):
    return pl.CostEstimate(flops=2 * macs, bytes_accessed=nbytes, transcendentals=0)


vmem = pl.BlockSpec(memory_space=pltpu.VMEM)
anywhere = pl.BlockSpec(memory_space=pl.ANY)


def shape(dims, dtype=bf16):
    return jax.ShapeDtypeStruct(dims, dtype)


def after(value, *earlier):
    return pl.pallas_call(
        lambda *refs: None,
        out_shape=shape(value.shape, value.dtype),
        in_specs=[anywhere] * (1 + len(earlier)),
        out_specs=anywhere,
        input_output_aliases={0: 0},
        compiler_params=limit(1),
    )(value, *earlier)


def share_kernel(value, out, done):
    rows = out.shape[0]
    place = lax.axis_index("rep") & 3
    here = pl.ds(pl.multiple_of(place * rows, rows), rows)
    copy = pltpu.make_async_copy(value.at[here], out, done)
    copy.start()
    copy.wait()


def share(value):
    return pl.pallas_call(
        share_kernel,
        out_shape=shape((value.shape[0] // 4, value.shape[1])),
        in_specs=[anywhere],
        out_specs=vmem,
        scratch_shapes=[pltpu.SemaphoreType.DMA],
        compiler_params=limit(1),
        cost_estimate=cost(3 * 10**9, value.size),
    )(value)


def assemble_kernel(pieces, out):
    rows = pieces[0].shape[0]
    for place in range(4):

        @pl.when((lax.axis_index("rep") & 3) == place)
        def _():
            for at, piece in enumerate(pieces):
                out[(place ^ at) * rows : ((place ^ at) + 1) * rows] = piece[...]


def normalized(tokens):
    values = tokens.astype(f32)
    center = values - jnp.mean(values, axis=1, keepdims=True)
    spread = jnp.mean(center * center, axis=1, keepdims=True)
    return (center * lax.rsqrt(spread + 1e-05)).astype(bf16)


def gelu_both(values):
    coeff = math.sqrt(2.0 / math.pi)
    square = values * values
    gate = 0.5 + 0.5 * jnp.tanh(coeff * values * (1.0 + 0.044715 * square))
    hidden = values * gate
    slope = gate + hidden * (1.0 - gate) * (2.0 * coeff + 6.0 * 0.044715 * coeff * square)
    return hidden.astype(bf16), slope.astype(bf16)


def forward_core(tokens, weights_in, weights_out, normed_t, slopes, part, base, total):
    count, width = tokens.shape
    block = weights_in[0].shape[1]
    tile = min(256, block)
    normed = normalized(tokens[...])
    normed_t[...] = normed.T
    for side in range(2):
        for at in range(0, block, tile):
            values = matmul(normed, weights_in[side][:, at : at + tile]) * (width**-0.5)
            hidden, slopes[side][:, at : at + tile] = gelu_both(values)
            term = matmul(hidden, weights_out[side][at : at + tile])
            if side + at == 0:
                total[...] = term
            else:
                total[...] += term
    part[...] = total[...].astype(bf16)
    values = tokens[...].astype(f32)
    ahead = pltpu.roll(values, count - 1, 0)
    rank = lax.broadcasted_iota(jnp.int32, values.shape, 0)
    base[...] = jnp.where(rank == count - 1, 0.0, total[...] + values - ahead)


def forward_kernel(pieces, skipped, *refs):
    given = refs[:pieces]
    own_in, mate_in, own_out, mate_out = refs[pieces : pieces + 4]
    normed_t, slope, slope_mate, part, base, total, tokens = refs[pieces + 4 + skipped :]
    if pieces > 1:
        assemble_kernel(given, tokens)
    else:
        tokens = given[0]
    weights = (own_in, mate_in), (own_out, mate_out)
    forward_core(tokens, *weights, normed_t, (slope, slope_mate), part, base, total)


def forward(given, count, weights, *earlier):
    width, block = weights[0].shape
    outs = (
        shape((width, count)),
        shape((count, block)),
        shape((count, block)),
        shape((count, width)),
        shape((count, width), f32),
    )
    return pl.pallas_call(
        functools.partial(forward_kernel, len(given), len(earlier)),
        out_shape=outs,
        in_specs=[vmem] * (len(given) + len(weights)) + [anywhere] * len(earlier),
        out_specs=[vmem for out in outs],
        scratch_shapes=[pltpu.VMEM((count, width), f32), pltpu.VMEM((count, width), bf16)],
        compiler_params=limit(12),
        cost_estimate=cost(0, 1000),
    )(*given, *weights, *earlier)


def errors_kernel(base, sent, *refs):
    errors = refs[-1]
    result = base[...] + sent[...].astype(f32)
    rank = lax.broadcasted_iota(jnp.int32, result.shape, 0)
    errors[...] = jnp.where(rank == result.shape[0] - 1, 0.0, result).astype(bf16)


def errors_of(base, sent, *earlier):
    return pl.pallas_call(
        errors_kernel,
        out_shape=shape(base.shape),
        in_specs=[vmem, vmem] + [anywhere] * len(earlier),
        out_specs=vmem,
        compiler_params=limit(2),
        cost_estimate=cost(0, 8 * base.size),
    )(base, sent, *earlier)


def strength_kernel(heat, out):
    out[...] = jnp.sqrt(jnp.full(out.shape, 2.0 * drift_stride * heat[0], f32))


def strength_of(heat, block):
    return pl.pallas_call(
        strength_kernel,
        out_shape=shape((1, block), f32),
        in_specs=[smem],
        out_specs=vmem,
        compiler_params=limit(1),
        cost_estimate=cost(0, 4 * block),
    )(heat)


def hidden_kernel(errors, weight, slope, *refs):
    out = refs[-1]
    tile = min(256, weight.shape[0])
    for at in range(0, weight.shape[0], tile):
        cols = slice(at, at + tile)
        product = against_rows(errors[...], weight[cols]) * slope[:, cols].astype(f32)
        out[:, cols] = product.astype(bf16)


def hidden_of(errors, weight, slope, *earlier):
    count, width = errors.shape
    block = weight.shape[0]
    return pl.pallas_call(
        hidden_kernel,
        out_shape=shape((count, block)),
        in_specs=[vmem] * 3 + [anywhere] * len(earlier),
        out_specs=vmem,
        compiler_params=limit(8),
        cost_estimate=cost(count * width * block, 2 * width * block),
    )(errors, weight, slope, *earlier)


def begin_kernel(strength, first, second, normed, normed_mate, params, noise, out):
    width = params.shape[1]
    rows = width // 4
    for start in range(0, width, rows):
        here = slice(start, start + rows)
        slope = matmul(normed[here], first[...]) + matmul(normed_mate[here], second[...])
        out[here] = (
            (1.0 - drift_stride) * params[0, here].astype(f32)
            + strength[...] * noise[0, here].astype(f32)
            - (drift_stride * width**-0.5) * slope
        )


def begin(strength, grads, normed, params, noise):
    width, count = normed[0].shape
    block = grads[0].shape[1]
    return pl.pallas_call(
        begin_kernel,
        out_shape=shape((width, block), f32),
        in_specs=[vmem] * 7,
        out_specs=vmem,
        compiler_params=limit(4),
        cost_estimate=cost(2 * width * count * block, 8 * width * count),
    )(strength, *grads, *normed, params, noise)


def update_kernel(start, begun, first, second, normed, normed_mate, *rest):
    out = rest[-1]
    here = slice(start, start + out.shape[0])
    slope = matmul(normed[here], first[...]) + matmul(normed_mate[here], second[...])
    out[...] = (begun[here] - (drift_stride * normed.shape[0] ** -0.5) * slope).astype(bf16)


def update(start, rows, begun, grads, normed, *earlier):
    count = normed[0].shape[1]
    block = grads[0].shape[1]
    return pl.pallas_call(
        functools.partial(update_kernel, start),
        out_shape=shape((rows, block)),
        in_specs=[vmem] * 5 + [anywhere] * len(earlier),
        out_specs=vmem,
        compiler_params=limit(4),
        cost_estimate=cost(2 * rows * count * block, 8 * rows * count),
    )(begun, *grads, *normed, *earlier)


def role(mate, swapped):
    rank = lax.axis_index("rep")
    odd = rank & 1
    taken = swapped[0] == 1
    return odd, taken & (mate[0] == rank + 1 - 2 * odd), taken & (mate[0] == rank - 1 + 2 * odd)


def finish_kernel(start, stop, count, mate, swapped, *refs):
    own, across, beyond = (refs[i * count : (i + 1) * count] for i in range(3))
    result, gaps, out, done = refs[-4:]
    odd, near_taken, far_taken = role(mate, swapped)
    at = 0
    for mine, near, far in zip(own, across, beyond):
        out[at : at + mine.shape[0]] = jnp.where(
            near_taken, near[...], jnp.where(far_taken, far[...], mine[...])
        )
        at += mine.shape[0]
    copy = pltpu.make_async_copy(out, result.at[0, pl.ds(start, stop - start)], done)
    copy.start()
    near_sum = far_sum = 0.0
    for part in range(count):
        mine, near, far = (pieces[part][...].astype(f32) for pieces in (own, across, beyond))
        near_sum += jnp.sum((near - mine) * (near - mine), axis=0, keepdims=True)
        far_sum += jnp.sum((far - mine) * (far - mine), axis=0, keepdims=True)
    if start > 0:
        so_far = refs[3 * count]
        near_sum += so_far[0, 0:1]
        far_sum += so_far[0, 1:2]
    if stop == result.shape[1]:
        near_sum *= 1.0 / result.shape[1]
        far_sum *= 1.0 / result.shape[1]
        near_sum, far_sum = (
            jnp.where(odd == 1, near_sum, far_sum),
            jnp.where(odd == 1, far_sum, near_sum),
        )
    gaps[0, 0:1] = near_sum
    gaps[0, 1:2] = far_sum
    copy.wait()


def finish(width, start, pairing, own, across, beyond, so_far):
    count = len(own)
    block = own[0].shape[1]
    stop = start + sum(value.shape[0] for value in own)
    given = [*own, *across, *beyond]
    specs = [vmem] * len(given)
    aliases = {}
    if start > 0:
        given += [so_far[1], so_far[0]]
        specs += [vmem, anywhere]
        aliases = {1 + len(given): 0}
    return pl.pallas_call(
        functools.partial(finish_kernel, start, stop, count),
        out_shape=(shape((1, width, block)), shape((1, 2, block), f32)),
        in_specs=[smem, smem] + specs,
        out_specs=(anywhere, vmem),
        scratch_shapes=[pltpu.VMEM((stop - start, block), bf16), pltpu.SemaphoreType.DMA],
        input_output_aliases=aliases,
        compiler_params=limit(4),
        cost_estimate=cost(0, 8 * (stop - start) * block),
    )(*pairing, *given)


def body(
    residual_flow,
    rooted_input_matrix,
    chain_normal_draws,
    output_matrix,
    chain_heat,
    matched_chain,
    swap_mask,
):
    replicas = lax.axis_size("rep")
    params = rooted_input_matrix[0]
    block = params.shape[1]
    count = residual_flow.shape[0]

    def to_core(value):
        return lax.ppermute(value, "dp", [(i, i ^ 1) for i in range(4)])

    def to_chip(value):
        return lax.ppermute(value, "dp", [(i, i ^ 2) for i in range(4)])

    def to_mate(value):
        return lax.ppermute(value, "rep", [(i, i ^ 1) for i in range(replicas)])

    def to_pair(value):
        return lax.ppermute(value, "rep", [(i, i ^ 2) for i in range(replicas)])

    def to_next(value):
        pairs = [(i, (i + (2 if i % 2 == 0 else -2)) % replicas) for i in range(replicas)]
        return lax.ppermute(value, "rep", pairs)

    def to_diagonal(value):
        return lax.ppermute(value, "rep", [(i, i ^ 3) for i in range(replicas)])

    mate_in = to_core(params)
    mate_out = to_core(output_matrix)
    token_share = share(residual_flow)
    token_own = to_chip(token_share)
    weights = (params, mate_in, output_matrix, mate_out)
    normed, slope, slope_send, part, base = forward((residual_flow,), count, weights)
    sent = to_chip(after(part, token_own))
    token_own = after(token_own, part)
    token_pieces = (token_own, to_mate(token_own), to_pair(token_own), to_diagonal(token_own))
    normed_mate = to_core(normed)
    far, far_slope, far_slope_send, far_part, far_base = forward(token_pieces, count, weights)
    far_sent = to_chip(far_part)
    far_mate = to_core(far)

    strength = strength_of(chain_heat, block)
    errors = errors_of(far_base, sent, normed_mate, strength)
    far_grads = [
        hidden_of(errors, output_matrix, far_slope),
        to_core(hidden_of(errors, mate_out, far_slope_send)),
    ]
    begun = begin(
        strength, far_grads, (far, far_mate), rooted_input_matrix, chain_normal_draws
    )
    errors = errors_of(base, far_sent, begun)
    grads = [
        hidden_of(errors, output_matrix, slope),
        to_core(hidden_of(errors, mate_out, slope_send)),
    ]

    pairing = (matched_chain, swap_mask)
    width = params.shape[0]
    sizes = [width * part // 64 for part in (13, 13, 13, 13, 12)]
    starts = [sum(sizes[:chunk]) for chunk in range(len(sizes))]
    own, across, beyond = [], [], []
    for chunk, (start, rows) in enumerate(zip(starts, sizes)):
        fresh = update(start, rows, begun, grads, (normed, normed_mate), *own[-1:])
        if chunk >= 3:
            fresh = after(fresh, across[chunk - 3])
        own.append(fresh)
        across.append(to_mate(fresh))
    for chunk in range(len(sizes)):
        if chunk >= 2:
            across[chunk] = after(across[chunk], beyond[chunk - 2])
        beyond.append(to_next(across[chunk]))
    done = None
    for first, stop in ((0, 4), (4, 5)):
        given = (pieces[first:stop] for pieces in (own, across, beyond))
        done = finish(width, starts[first], pairing, *given, done)
    return done


def solution(mesh):
    placed = (
        P("dp", None),
        P("rep", None, "dp"),
        P("rep", None, "dp"),
        P("dp", None),
        P("rep"),
        P("rep"),
        P("rep"),
    )
    return jax.shard_map(
        body,
        mesh=mesh,
        in_specs=placed,
        out_specs=(P("rep", None, "dp"), P("rep", None, "dp")),
        check_vma=False,
    )
```

```python
import functools
import math

import jax
import jax.numpy as jnp
from jax import lax
from jax.experimental import pallas as pl
from jax.experimental.pallas import tpu as pltpu
from jax.sharding import PartitionSpec as P

drift_stride = 0.5
f32 = jnp.float32
bf16 = jnp.bfloat16
smem = pl.BlockSpec(memory_space=pltpu.SMEM)


def matmul(left, right):
    return jnp.dot(left, right, preferred_element_type=f32)


def against_rows(left, right):
    return lax.dot_general(left, right, (((1,), (1,)), ((), ())), preferred_element_type=f32)


def limit(mebibytes):
    return pltpu.CompilerParams(vmem_limit_bytes=mebibytes * 1024 * 1024)


def cost(macs, nbytes):
    return pl.CostEstimate(flops=2 * macs, bytes_accessed=nbytes, transcendentals=0)


vmem = pl.BlockSpec(memory_space=pltpu.VMEM)
anywhere = pl.BlockSpec(memory_space=pl.ANY)


def shape(dims, dtype=bf16):
    return jax.ShapeDtypeStruct(dims, dtype)


def after(value, *earlier):
    return pl.pallas_call(
        lambda *refs: None,
        out_shape=shape(value.shape, value.dtype),
        in_specs=[anywhere] * (1 + len(earlier)),
        out_specs=anywhere,
        input_output_aliases={0: 0},
        compiler_params=limit(1),
    )(value, *earlier)


def share_kernel(value, out, done):
    rows = out.shape[0]
    place = lax.axis_index("rep") & 3
    here = pl.ds(pl.multiple_of(place * rows, rows), rows)
    copy = pltpu.make_async_copy(value.at[here], out, done)
    copy.start()
    copy.wait()


def share(value):
    return pl.pallas_call(
        share_kernel,
        out_shape=shape((value.shape[0] // 4, value.shape[1])),
        in_specs=[anywhere],
        out_specs=vmem,
        scratch_shapes=[pltpu.SemaphoreType.DMA],
        compiler_params=limit(1),
        cost_estimate=cost(3 * 10**9, value.size),
    )(value)


def assemble_kernel(pieces, out):
    rows = pieces[0].shape[0]
    for place in range(4):

        @pl.when((lax.axis_index("rep") & 3) == place)
        def _():
            for at, piece in enumerate(pieces):
                out[(place ^ at) * rows : ((place ^ at) + 1) * rows] = piece[...]


def normalized(tokens):
    values = tokens.astype(f32)
    center = values - jnp.mean(values, axis=1, keepdims=True)
    spread = jnp.mean(center * center, axis=1, keepdims=True)
    return (center * lax.rsqrt(spread + 1e-05)).astype(bf16)


def gelu_both(values):
    coeff = math.sqrt(2.0 / math.pi)
    square = values * values
    gate = 0.5 + 0.5 * jnp.tanh(coeff * values * (1.0 + 0.044715 * square))
    hidden = values * gate
    slope = gate + hidden * (1.0 - gate) * (2.0 * coeff + 6.0 * 0.044715 * coeff * square)
    return hidden.astype(bf16), slope.astype(bf16)


def forward_core(tokens, weights_in, weights_out, normed_t, slopes, part, base, total):
    count, width = tokens.shape
    block = weights_in[0].shape[1]
    tile = min(256, block)
    normed = normalized(tokens[...])
    normed_t[...] = normed.T
    for side in range(2):
        for at in range(0, block, tile):
            values = matmul(normed, weights_in[side][:, at : at + tile]) * (width**-0.5)
            hidden, slopes[side][:, at : at + tile] = gelu_both(values)
            term = matmul(hidden, weights_out[side][at : at + tile])
            if side + at == 0:
                total[...] = term
            else:
                total[...] += term
    part[...] = total[...].astype(bf16)
    values = tokens[...].astype(f32)
    ahead = pltpu.roll(values, count - 1, 0)
    rank = lax.broadcasted_iota(jnp.int32, values.shape, 0)
    base[...] = jnp.where(rank == count - 1, 0.0, total[...] + values - ahead)


def forward_kernel(pieces, skipped, *refs):
    given = refs[:pieces]
    own_in, mate_in, own_out, mate_out = refs[pieces : pieces + 4]
    normed_t, slope, slope_mate, part, base, total, tokens = refs[pieces + 4 + skipped :]
    if pieces > 1:
        assemble_kernel(given, tokens)
    else:
        tokens = given[0]
    weights = (own_in, mate_in), (own_out, mate_out)
    forward_core(tokens, *weights, normed_t, (slope, slope_mate), part, base, total)


def forward(given, count, weights, *earlier):
    width, block = weights[0].shape
    outs = (
        shape((width, count)),
        shape((count, block)),
        shape((count, block)),
        shape((count, width)),
        shape((count, width), f32),
    )
    return pl.pallas_call(
        functools.partial(forward_kernel, len(given), len(earlier)),
        out_shape=outs,
        in_specs=[vmem] * (len(given) + len(weights)) + [anywhere] * len(earlier),
        out_specs=[vmem for out in outs],
        scratch_shapes=[pltpu.VMEM((count, width), f32), pltpu.VMEM((count, width), bf16)],
        compiler_params=limit(12),
        cost_estimate=cost(0, 1000),
    )(*given, *weights, *earlier)


def errors_kernel(base, sent, *refs):
    errors = refs[-1]
    result = base[...] + sent[...].astype(f32)
    rank = lax.broadcasted_iota(jnp.int32, result.shape, 0)
    errors[...] = jnp.where(rank == result.shape[0] - 1, 0.0, result).astype(bf16)


def errors_of(base, sent, *earlier):
    return pl.pallas_call(
        errors_kernel,
        out_shape=shape(base.shape),
        in_specs=[vmem, vmem] + [anywhere] * len(earlier),
        out_specs=vmem,
        compiler_params=limit(2),
        cost_estimate=cost(0, 8 * base.size),
    )(base, sent, *earlier)


def strength_kernel(heat, out):
    out[...] = jnp.sqrt(jnp.full(out.shape, 2.0 * drift_stride * heat[0], f32))


def strength_of(heat, block):
    return pl.pallas_call(
        strength_kernel,
        out_shape=shape((1, block), f32),
        in_specs=[smem],
        out_specs=vmem,
        compiler_params=limit(1),
        cost_estimate=cost(0, 4 * block),
    )(heat)


def hidden_kernel(errors, weight, slope, *refs):
    out = refs[-1]
    tile = min(256, weight.shape[0])
    for at in range(0, weight.shape[0], tile):
        cols = slice(at, at + tile)
        product = against_rows(errors[...], weight[cols]) * slope[:, cols].astype(f32)
        out[:, cols] = product.astype(bf16)


def hidden_of(errors, weight, slope, *earlier):
    count, width = errors.shape
    block = weight.shape[0]
    return pl.pallas_call(
        hidden_kernel,
        out_shape=shape((count, block)),
        in_specs=[vmem] * 3 + [anywhere] * len(earlier),
        out_specs=vmem,
        compiler_params=limit(8),
        cost_estimate=cost(count * width * block, 2 * width * block),
    )(errors, weight, slope, *earlier)


def begin_kernel(strength, first, second, normed, normed_mate, params, noise, out):
    width = params.shape[1]
    rows = width // 4
    for start in range(0, width, rows):
        here = slice(start, start + rows)
        slope = matmul(normed[here], first[...]) + matmul(normed_mate[here], second[...])
        out[here] = (
            (1.0 - drift_stride) * params[0, here].astype(f32)
            + strength[...] * noise[0, here].astype(f32)
            - (drift_stride * width**-0.5) * slope
        )


def begin(strength, grads, normed, params, noise):
    width, count = normed[0].shape
    block = grads[0].shape[1]
    return pl.pallas_call(
        begin_kernel,
        out_shape=shape((width, block), f32),
        in_specs=[vmem] * 7,
        out_specs=vmem,
        compiler_params=limit(4),
        cost_estimate=cost(2 * width * count * block, 8 * width * count),
    )(strength, *grads, *normed, params, noise)


def update_kernel(start, begun, first, second, normed, normed_mate, *rest):
    out = rest[-1]
    here = slice(start, start + out.shape[0])
    slope = matmul(normed[here], first[...]) + matmul(normed_mate[here], second[...])
    out[...] = (begun[here] - (drift_stride * normed.shape[0] ** -0.5) * slope).astype(bf16)


def update(start, rows, begun, grads, normed, *earlier):
    count = normed[0].shape[1]
    block = grads[0].shape[1]
    return pl.pallas_call(
        functools.partial(update_kernel, start),
        out_shape=shape((rows, block)),
        in_specs=[vmem] * 5 + [anywhere] * len(earlier),
        out_specs=vmem,
        compiler_params=limit(4),
        cost_estimate=cost(2 * rows * count * block, 8 * rows * count),
    )(begun, *grads, *normed, *earlier)


def role(mate, swapped):
    rank = lax.axis_index("rep")
    odd = rank & 1
    taken = swapped[0] == 1
    return odd, taken & (mate[0] == rank + 1 - 2 * odd), taken & (mate[0] == rank - 1 + 2 * odd)


def finish_kernel(start, stop, count, mate, swapped, *refs):
    own, across, beyond = (refs[i * count : (i + 1) * count] for i in range(3))
    result, gaps, out, done = refs[-4:]
    odd, near_taken, far_taken = role(mate, swapped)
    at = 0
    for mine, near, far in zip(own, across, beyond):
        out[at : at + mine.shape[0]] = jnp.where(
            near_taken, near[...], jnp.where(far_taken, far[...], mine[...])
        )
        at += mine.shape[0]
    copy = pltpu.make_async_copy(out, result.at[0, pl.ds(start, stop - start)], done)
    copy.start()
    near_sum = far_sum = 0.0
    for part in range(count):
        mine, near, far = (pieces[part][...].astype(f32) for pieces in (own, across, beyond))
        near_sum += jnp.sum((near - mine) * (near - mine), axis=0, keepdims=True)
        far_sum += jnp.sum((far - mine) * (far - mine), axis=0, keepdims=True)
    if start > 0:
        so_far = refs[3 * count]
        near_sum += so_far[0, 0:1]
        far_sum += so_far[0, 1:2]
    if stop == result.shape[1]:
        near_sum *= 1.0 / result.shape[1]
        far_sum *= 1.0 / result.shape[1]
        near_sum, far_sum = (
            jnp.where(odd == 1, near_sum, far_sum),
            jnp.where(odd == 1, far_sum, near_sum),
        )
    gaps[0, 0:1] = near_sum
    gaps[0, 1:2] = far_sum
    copy.wait()


def finish(width, start, pairing, own, across, beyond, so_far):
    count = len(own)
    block = own[0].shape[1]
    stop = start + sum(value.shape[0] for value in own)
    given = [*own, *across, *beyond]
    specs = [vmem] * len(given)
    aliases = {}
    if start > 0:
        given += [so_far[1], so_far[0]]
        specs += [vmem, anywhere]
        aliases = {1 + len(given): 0}
    return pl.pallas_call(
        functools.partial(finish_kernel, start, stop, count),
        out_shape=(shape((1, width, block)), shape((1, 2, block), f32)),
        in_specs=[smem, smem] + specs,
        out_specs=(anywhere, vmem),
        scratch_shapes=[pltpu.VMEM((stop - start, block), bf16), pltpu.SemaphoreType.DMA],
        input_output_aliases=aliases,
        compiler_params=limit(4),
        cost_estimate=cost(0, 8 * (stop - start) * block),
    )(*pairing, *given)


def body(
    residual_flow,
    rooted_input_matrix,
    chain_normal_draws,
    output_matrix,
    chain_heat,
    matched_chain,
    swap_mask,
):
    replicas = lax.axis_size("rep")
    params = rooted_input_matrix[0]
    block = params.shape[1]
    count = residual_flow.shape[0]

    def to_core(value):
        return lax.ppermute(value, "dp", [(i, i ^ 1) for i in range(4)])

    def to_chip(value):
        return lax.ppermute(value, "dp", [(i, i ^ 2) for i in range(4)])

    def to_mate(value):
        return lax.ppermute(value, "rep", [(i, i ^ 1) for i in range(replicas)])

    def to_pair(value):
        return lax.ppermute(value, "rep", [(i, i ^ 2) for i in range(replicas)])

    def to_next(value):
        pairs = [(i, (i + (2 if i % 2 == 0 else -2)) % replicas) for i in range(replicas)]
        return lax.ppermute(value, "rep", pairs)

    def to_diagonal(value):
        return lax.ppermute(value, "rep", [(i, i ^ 3) for i in range(replicas)])

    mate_in = to_core(params)
    mate_out = to_core(output_matrix)
    token_share = share(residual_flow)
    token_own = to_chip(token_share)
    weights = (params, mate_in, output_matrix, mate_out)
    normed, slope, slope_send, part, base = forward((residual_flow,), count, weights)
    sent = to_chip(after(part, token_own))
    token_own = after(token_own, part)
    token_pieces = (token_own, to_mate(token_own), to_pair(token_own), to_diagonal(token_own))
    normed_mate = to_core(normed)
    far, far_slope, far_slope_send, far_part, far_base = forward(token_pieces, count, weights)
    far_sent = to_chip(far_part)
    far_mate = to_core(far)

    strength = strength_of(chain_heat, block)
    errors = errors_of(far_base, sent, normed_mate, strength)
    far_grads = [
        hidden_of(errors, output_matrix, far_slope),
        to_core(hidden_of(errors, mate_out, far_slope_send)),
    ]
    begun = begin(
        strength, far_grads, (far, far_mate), rooted_input_matrix, chain_normal_draws
    )
    errors = errors_of(base, far_sent, begun)
    grads = [
        hidden_of(errors, output_matrix, slope),
        to_core(hidden_of(errors, mate_out, slope_send)),
    ]

    pairing = (matched_chain, swap_mask)
    width = params.shape[0]
    sizes = [width * part // 64 for part in (13, 13, 13, 13, 12)]
    starts = [sum(sizes[:chunk]) for chunk in range(len(sizes))]
    fresh = []
    for start, rows in zip(starts, sizes):
        fresh.append(update(start, rows, begun, grads, (normed, normed_mate), *fresh[-1:]))
    own, across, beyond = [], [], []
    for chunk, piece in enumerate(fresh):
        earlier = across[chunk - 3 : chunk - 3 + 1] if chunk >= 3 else []
        if chunk == 1:
            earlier = [*earlier, fresh[-1]]
        own.append(after(piece, *earlier) if earlier else piece)
        across.append(to_mate(own[-1]))
    for chunk in range(len(sizes)):
        if chunk >= 2:
            across[chunk] = after(across[chunk], beyond[chunk - 2])
        beyond.append(to_next(across[chunk]))
    done = None
    for first, stop in ((0, 4), (4, 5)):
        given = (pieces[first:stop] for pieces in (own, across, beyond))
        done = finish(width, starts[first], pairing, *given, done)
    return done


def solution(mesh):
    placed = (
        P("dp", None),
        P("rep", None, "dp"),
        P("rep", None, "dp"),
        P("dp", None),
        P("rep"),
        P("rep"),
        P("rep"),
    )
    return jax.shard_map(
        body,
        mesh=mesh,
        in_specs=placed,
        out_specs=(P("rep", None, "dp"), P("rep", None, "dp")),
        check_vma=False,
    )
```

```python
import functools
import math

import jax
import jax.numpy as jnp
from jax import lax
from jax.experimental import pallas as pl
from jax.experimental.pallas import tpu as pltpu
from jax.sharding import PartitionSpec as P

drift_stride = 0.5
f32 = jnp.float32
bf16 = jnp.bfloat16
smem = pl.BlockSpec(memory_space=pltpu.SMEM)


def matmul(left, right):
    return jnp.dot(left, right, preferred_element_type=f32)


def against_rows(left, right):
    return lax.dot_general(left, right, (((1,), (1,)), ((), ())), preferred_element_type=f32)


def limit(mebibytes):
    return pltpu.CompilerParams(vmem_limit_bytes=mebibytes * 1024 * 1024)


def cost(macs, nbytes):
    return pl.CostEstimate(flops=2 * macs, bytes_accessed=nbytes, transcendentals=0)


vmem = pl.BlockSpec(memory_space=pltpu.VMEM)
anywhere = pl.BlockSpec(memory_space=pl.ANY)


def shape(dims, dtype=bf16):
    return jax.ShapeDtypeStruct(dims, dtype)


def after(value, *earlier):
    return pl.pallas_call(
        lambda *refs: None,
        out_shape=shape(value.shape, value.dtype),
        in_specs=[anywhere] * (1 + len(earlier)),
        out_specs=anywhere,
        input_output_aliases={0: 0},
        compiler_params=limit(1),
    )(value, *earlier)


def share_kernel(value, out, done):
    rows = out.shape[0]
    place = lax.axis_index("rep") & 3
    here = pl.ds(pl.multiple_of(place * rows, rows), rows)
    copy = pltpu.make_async_copy(value.at[here], out, done)
    copy.start()
    copy.wait()


def share(value):
    return pl.pallas_call(
        share_kernel,
        out_shape=shape((value.shape[0] // 4, value.shape[1])),
        in_specs=[anywhere],
        out_specs=vmem,
        scratch_shapes=[pltpu.SemaphoreType.DMA],
        compiler_params=limit(1),
        cost_estimate=cost(3 * 10**9, value.size),
    )(value)


def assemble_kernel(pieces, out):
    rows = pieces[0].shape[0]
    for place in range(4):

        @pl.when((lax.axis_index("rep") & 3) == place)
        def _():
            for at, piece in enumerate(pieces):
                out[(place ^ at) * rows : ((place ^ at) + 1) * rows] = piece[...]


def normalized(tokens):
    values = tokens.astype(f32)
    center = values - jnp.mean(values, axis=1, keepdims=True)
    spread = jnp.mean(center * center, axis=1, keepdims=True)
    return (center * lax.rsqrt(spread + 1e-05)).astype(bf16)


def gelu_both(values):
    coeff = math.sqrt(2.0 / math.pi)
    square = values * values
    gate = 0.5 + 0.5 * jnp.tanh(coeff * values * (1.0 + 0.044715 * square))
    hidden = values * gate
    slope = gate + hidden * (1.0 - gate) * (2.0 * coeff + 6.0 * 0.044715 * coeff * square)
    return hidden.astype(bf16), slope.astype(bf16)


def forward_core(tokens, weights_in, weights_out, normed_t, slopes, part, base, total):
    count, width = tokens.shape
    block = weights_in[0].shape[1]
    tile = min(256, block)
    normed = normalized(tokens[...])
    normed_t[...] = normed.T
    for side in range(2):
        for at in range(0, block, tile):
            values = matmul(normed, weights_in[side][:, at : at + tile]) * (width**-0.5)
            hidden, slopes[side][:, at : at + tile] = gelu_both(values)
            term = matmul(hidden, weights_out[side][at : at + tile])
            if side + at == 0:
                total[...] = term
            else:
                total[...] += term
    part[...] = total[...].astype(bf16)
    values = tokens[...].astype(f32)
    ahead = pltpu.roll(values, count - 1, 0)
    rank = lax.broadcasted_iota(jnp.int32, values.shape, 0)
    base[...] = jnp.where(rank == count - 1, 0.0, total[...] + values - ahead)


def forward_kernel(pieces, skipped, *refs):
    given = refs[:pieces]
    own_in, mate_in, own_out, mate_out = refs[pieces : pieces + 4]
    normed_t, slope, slope_mate, part, base, total, tokens = refs[pieces + 4 + skipped :]
    if pieces > 1:
        assemble_kernel(given, tokens)
    else:
        tokens = given[0]
    weights = (own_in, mate_in), (own_out, mate_out)
    forward_core(tokens, *weights, normed_t, (slope, slope_mate), part, base, total)


def forward(given, count, weights, *earlier):
    width, block = weights[0].shape
    outs = (
        shape((width, count)),
        shape((count, block)),
        shape((count, block)),
        shape((count, width)),
        shape((count, width), f32),
    )
    return pl.pallas_call(
        functools.partial(forward_kernel, len(given), len(earlier)),
        out_shape=outs,
        in_specs=[vmem] * (len(given) + len(weights)) + [anywhere] * len(earlier),
        out_specs=[vmem for out in outs],
        scratch_shapes=[pltpu.VMEM((count, width), f32), pltpu.VMEM((count, width), bf16)],
        compiler_params=limit(12),
        cost_estimate=cost(0, 1000),
    )(*given, *weights, *earlier)


def errors_kernel(base, sent, *refs):
    errors = refs[-1]
    result = base[...] + sent[...].astype(f32)
    rank = lax.broadcasted_iota(jnp.int32, result.shape, 0)
    errors[...] = jnp.where(rank == result.shape[0] - 1, 0.0, result).astype(bf16)


def errors_of(base, sent, *earlier):
    return pl.pallas_call(
        errors_kernel,
        out_shape=shape(base.shape),
        in_specs=[vmem, vmem] + [anywhere] * len(earlier),
        out_specs=vmem,
        compiler_params=limit(2),
        cost_estimate=cost(0, 8 * base.size),
    )(base, sent, *earlier)


def strength_kernel(heat, out):
    out[...] = jnp.sqrt(jnp.full(out.shape, 2.0 * drift_stride * heat[0], f32))


def strength_of(heat, block):
    return pl.pallas_call(
        strength_kernel,
        out_shape=shape((1, block), f32),
        in_specs=[smem],
        out_specs=vmem,
        compiler_params=limit(1),
        cost_estimate=cost(0, 4 * block),
    )(heat)


def hidden_kernel(errors, weight, slope, *refs):
    out = refs[-1]
    tile = min(256, weight.shape[0])
    for at in range(0, weight.shape[0], tile):
        cols = slice(at, at + tile)
        product = against_rows(errors[...], weight[cols]) * slope[:, cols].astype(f32)
        out[:, cols] = product.astype(bf16)


def hidden_of(errors, weight, slope, *earlier):
    count, width = errors.shape
    block = weight.shape[0]
    return pl.pallas_call(
        hidden_kernel,
        out_shape=shape((count, block)),
        in_specs=[vmem] * 3 + [anywhere] * len(earlier),
        out_specs=vmem,
        compiler_params=limit(8),
        cost_estimate=cost(count * width * block, 2 * width * block),
    )(errors, weight, slope, *earlier)


def send_kernel(base, sent, weight, slope, order, errors, grad):
    errors_kernel(base, sent, errors)
    hidden_kernel(errors, weight, slope, grad)


def send_of(base, sent, weight, slope, order):
    count, block = slope.shape
    return pl.pallas_call(
        send_kernel,
        out_shape=(shape(base.shape), shape((count, block))),
        in_specs=[vmem] * 4 + [anywhere],
        out_specs=(vmem, vmem),
        compiler_params=limit(8),
        cost_estimate=cost(base.size * block, 8 * base.size),
    )(base, sent, weight, slope, order)


def carry_kernel(begun, errors, weight, slope, normed, out, grad):
    hidden_kernel(errors, weight, slope, grad)
    width = normed.shape[0]
    rows = width // 4
    scale = drift_stride * width**-0.5
    for start in range(0, width, rows):
        here = slice(start, start + rows)
        out[here] = begun[here] - scale * matmul(normed[here], grad[...])


def carry(begun, errors, weight, slope, normed):
    return pl.pallas_call(
        carry_kernel,
        out_shape=shape(begun.shape, f32),
        in_specs=[vmem] * 5,
        out_specs=vmem,
        scratch_shapes=[pltpu.VMEM(slope.shape, bf16)],
        compiler_params=limit(8),
        cost_estimate=cost(2 * errors.size * slope.shape[1], 8 * begun.size),
    )(begun, errors, weight, slope, normed)


def begin_kernel(strength, first, second, normed, normed_mate, params, noise, out):
    width = params.shape[1]
    rows = width // 4
    for start in range(0, width, rows):
        here = slice(start, start + rows)
        slope = matmul(normed[here], first[...]) + matmul(normed_mate[here], second[...])
        out[here] = (
            (1.0 - drift_stride) * params[0, here].astype(f32)
            + strength[...] * noise[0, here].astype(f32)
            - (drift_stride * width**-0.5) * slope
        )


def begin(strength, grads, normed, params, noise):
    width, count = normed[0].shape
    block = grads[0].shape[1]
    return pl.pallas_call(
        begin_kernel,
        out_shape=shape((width, block), f32),
        in_specs=[vmem] * 7,
        out_specs=vmem,
        compiler_params=limit(4),
        cost_estimate=cost(2 * width * count * block, 8 * width * count),
    )(strength, *grads, *normed, params, noise)


def update_kernel(start, begun, grad, normed, *rest):
    out = rest[-1]
    here = slice(start, start + out.shape[0])
    slope = matmul(normed[here], grad[...])
    out[...] = (begun[here] - (drift_stride * normed.shape[0] ** -0.5) * slope).astype(bf16)


def update(start, rows, begun, grad, normed, *earlier):
    count, block = grad.shape
    return pl.pallas_call(
        functools.partial(update_kernel, start),
        out_shape=shape((rows, block)),
        in_specs=[vmem] * 3 + [anywhere] * len(earlier),
        out_specs=vmem,
        compiler_params=limit(4),
        cost_estimate=cost(rows * count * block, 8 * rows * count),
    )(begun, grad, normed, *earlier)


def role(mate, swapped):
    rank = lax.axis_index("rep")
    odd = rank & 1
    taken = swapped[0] == 1
    return odd, taken & (mate[0] == rank + 1 - 2 * odd), taken & (mate[0] == rank - 1 + 2 * odd)


def finish_kernel(start, stop, count, mate, swapped, *refs):
    own, across, beyond = (refs[i * count : (i + 1) * count] for i in range(3))
    result, gaps, out, done = refs[-4:]
    odd, near_taken, far_taken = role(mate, swapped)
    at = 0
    for mine, near, far in zip(own, across, beyond):
        out[at : at + mine.shape[0]] = jnp.where(
            near_taken, near[...], jnp.where(far_taken, far[...], mine[...])
        )
        at += mine.shape[0]
    copy = pltpu.make_async_copy(out, result.at[0, pl.ds(start, stop - start)], done)
    copy.start()
    near_sum = far_sum = 0.0
    for part in range(count):
        mine, near, far = (pieces[part][...].astype(f32) for pieces in (own, across, beyond))
        near_sum += jnp.sum((near - mine) * (near - mine), axis=0, keepdims=True)
        far_sum += jnp.sum((far - mine) * (far - mine), axis=0, keepdims=True)
    if start > 0:
        so_far = refs[3 * count]
        near_sum += so_far[0, 0:1]
        far_sum += so_far[0, 1:2]
    if stop == result.shape[1]:
        near_sum *= 1.0 / result.shape[1]
        far_sum *= 1.0 / result.shape[1]
        near_sum, far_sum = (
            jnp.where(odd == 1, near_sum, far_sum),
            jnp.where(odd == 1, far_sum, near_sum),
        )
    gaps[0, 0:1] = near_sum
    gaps[0, 1:2] = far_sum
    copy.wait()


def finish(width, start, pairing, own, across, beyond, so_far):
    count = len(own)
    block = own[0].shape[1]
    stop = start + sum(value.shape[0] for value in own)
    given = [*own, *across, *beyond]
    specs = [vmem] * len(given)
    aliases = {}
    if start > 0:
        given += [so_far[1], so_far[0]]
        specs += [vmem, anywhere]
        aliases = {1 + len(given): 0}
    return pl.pallas_call(
        functools.partial(finish_kernel, start, stop, count),
        out_shape=(shape((1, width, block)), shape((1, 2, block), f32)),
        in_specs=[smem, smem] + specs,
        out_specs=(anywhere, vmem),
        scratch_shapes=[pltpu.VMEM((stop - start, block), bf16), pltpu.SemaphoreType.DMA],
        input_output_aliases=aliases,
        compiler_params=limit(4),
        cost_estimate=cost(0, 8 * (stop - start) * block),
    )(*pairing, *given)


def body(
    residual_flow,
    rooted_input_matrix,
    chain_normal_draws,
    output_matrix,
    chain_heat,
    matched_chain,
    swap_mask,
):
    replicas = lax.axis_size("rep")
    params = rooted_input_matrix[0]
    block = params.shape[1]
    count = residual_flow.shape[0]

    def to_core(value):
        return lax.ppermute(value, "dp", [(i, i ^ 1) for i in range(4)])

    def to_chip(value):
        return lax.ppermute(value, "dp", [(i, i ^ 2) for i in range(4)])

    def to_mate(value):
        return lax.ppermute(value, "rep", [(i, i ^ 1) for i in range(replicas)])

    def to_pair(value):
        return lax.ppermute(value, "rep", [(i, i ^ 2) for i in range(replicas)])

    def to_next(value):
        pairs = [(i, (i + (2 if i % 2 == 0 else -2)) % replicas) for i in range(replicas)]
        return lax.ppermute(value, "rep", pairs)

    def to_diagonal(value):
        return lax.ppermute(value, "rep", [(i, i ^ 3) for i in range(replicas)])

    mate_in = to_core(params)
    mate_out = to_core(output_matrix)
    token_share = share(residual_flow)
    token_own = to_chip(token_share)
    weights = (params, mate_in, output_matrix, mate_out)
    normed, slope, slope_send, part, base = forward((residual_flow,), count, weights)
    sent = to_chip(after(part, token_own))
    token_own = after(token_own, part)
    token_pieces = (token_own, to_mate(token_own), to_pair(token_own), to_diagonal(token_own))
    normed_mate = to_core(normed)
    far, far_slope, far_slope_send, far_part, far_base = forward(token_pieces, count, weights)
    far_sent = to_chip(far_part)
    far_mate = to_core(far)

    strength = strength_of(chain_heat, block)
    errors = errors_of(far_base, sent, normed_mate, strength)
    far_grads = [
        hidden_of(errors, output_matrix, far_slope),
        to_core(hidden_of(errors, mate_out, far_slope_send)),
    ]
    begun = begin(
        strength, far_grads, (far, far_mate), rooted_input_matrix, chain_normal_draws
    )
    errors, grad = send_of(base, far_sent, mate_out, slope_send, begun)
    begun = carry(begun, errors, output_matrix, slope, normed)
    grad = to_core(grad)

    pairing = (matched_chain, swap_mask)
    width = params.shape[0]
    sizes = [width * part // 64 for part in (13, 13, 13, 13, 12)]
    starts = [sum(sizes[:chunk]) for chunk in range(len(sizes))]
    fresh = []
    for start, rows in zip(starts, sizes):
        fresh.append(update(start, rows, begun, grad, normed_mate, *fresh[-1:]))
    own, across, beyond = [], [], []
    for chunk, piece in enumerate(fresh):
        earlier = across[chunk - 3 : chunk - 3 + 1] if chunk >= 3 else []
        if chunk == 1:
            earlier = [*earlier, fresh[-1]]
        own.append(after(piece, *earlier) if earlier else piece)
        across.append(to_mate(own[-1]))
    for chunk in range(len(sizes)):
        if chunk >= 2:
            across[chunk] = after(across[chunk], beyond[chunk - 2])
        beyond.append(to_next(across[chunk]))
    done = None
    for first, stop in ((0, 4), (4, 5)):
        given = (pieces[first:stop] for pieces in (own, across, beyond))
        done = finish(width, starts[first], pairing, *given, done)
    return done


def solution(mesh):
    placed = (
        P("dp", None),
        P("rep", None, "dp"),
        P("rep", None, "dp"),
        P("dp", None),
        P("rep"),
        P("rep"),
        P("rep"),
    )
    return jax.shard_map(
        body,
        mesh=mesh,
        in_specs=placed,
        out_specs=(P("rep", None, "dp"), P("rep", None, "dp")),
        check_vma=False,
    )
```

```python
import functools
import math

import jax
import jax.numpy as jnp
from jax import lax
from jax.experimental import pallas as pl
from jax.experimental.pallas import tpu as pltpu
from jax.sharding import PartitionSpec as P

drift_stride = 0.5
f32 = jnp.float32
bf16 = jnp.bfloat16
smem = pl.BlockSpec(memory_space=pltpu.SMEM)


def matmul(left, right):
    return jnp.dot(left, right, preferred_element_type=f32)


def against_rows(left, right):
    return lax.dot_general(left, right, (((1,), (1,)), ((), ())), preferred_element_type=f32)


def limit(mebibytes):
    return pltpu.CompilerParams(vmem_limit_bytes=mebibytes * 1024 * 1024)


def cost(macs, nbytes):
    return pl.CostEstimate(flops=2 * macs, bytes_accessed=nbytes, transcendentals=0)


vmem = pl.BlockSpec(memory_space=pltpu.VMEM)
anywhere = pl.BlockSpec(memory_space=pl.ANY)


def shape(dims, dtype=bf16):
    return jax.ShapeDtypeStruct(dims, dtype)


def after(value, *earlier):
    return pl.pallas_call(
        lambda *refs: None,
        out_shape=shape(value.shape, value.dtype),
        in_specs=[anywhere] * (1 + len(earlier)),
        out_specs=anywhere,
        input_output_aliases={0: 0},
        compiler_params=limit(1),
    )(value, *earlier)


def share_kernel(value, out, done):
    rows = out.shape[0]
    place = lax.axis_index("rep") & 3
    here = pl.ds(pl.multiple_of(place * rows, rows), rows)
    copy = pltpu.make_async_copy(value.at[here], out, done)
    copy.start()
    copy.wait()


def share(value):
    return pl.pallas_call(
        share_kernel,
        out_shape=shape((value.shape[0] // 4, value.shape[1])),
        in_specs=[anywhere],
        out_specs=vmem,
        scratch_shapes=[pltpu.SemaphoreType.DMA],
        compiler_params=limit(1),
        cost_estimate=cost(3 * 10**9, value.size),
    )(value)


def assemble_kernel(pieces, out):
    rows = pieces[0].shape[0]
    for place in range(4):

        @pl.when((lax.axis_index("rep") & 3) == place)
        def _():
            for at, piece in enumerate(pieces):
                out[(place ^ at) * rows : ((place ^ at) + 1) * rows] = piece[...]


def normalized(tokens):
    values = tokens.astype(f32)
    center = values - jnp.mean(values, axis=1, keepdims=True)
    spread = jnp.mean(center * center, axis=1, keepdims=True)
    return (center * lax.rsqrt(spread + 1e-05)).astype(bf16)


def gelu_both(values):
    coeff = math.sqrt(2.0 / math.pi)
    square = values * values
    gate = 0.5 + 0.5 * jnp.tanh(coeff * values * (1.0 + 0.044715 * square))
    hidden = values * gate
    slope = gate + hidden * (1.0 - gate) * (2.0 * coeff + 6.0 * 0.044715 * coeff * square)
    return hidden.astype(bf16), slope.astype(bf16)


def forward_core(tokens, weights_in, weights_out, normed_t, slopes, part, base, total):
    count, width = tokens.shape
    block = weights_in[0].shape[1]
    tile = min(256, block)
    normed = normalized(tokens[...])
    normed_t[...] = normed.T
    for side in range(2):
        for at in range(0, block, tile):
            values = matmul(normed, weights_in[side][:, at : at + tile]) * (width**-0.5)
            hidden, slopes[side][:, at : at + tile] = gelu_both(values)
            term = matmul(hidden, weights_out[side][at : at + tile])
            if side + at == 0:
                total[...] = term
            else:
                total[...] += term
    part[...] = total[...].astype(bf16)
    values = tokens[...].astype(f32)
    ahead = pltpu.roll(values, count - 1, 0)
    rank = lax.broadcasted_iota(jnp.int32, values.shape, 0)
    base[...] = jnp.where(rank == count - 1, 0.0, total[...] + values - ahead)


def forward_kernel(pieces, skipped, *refs):
    given = refs[:pieces]
    own_in, mate_in, own_out, mate_out = refs[pieces : pieces + 4]
    normed_t, slope, slope_mate, part, base, total, tokens = refs[pieces + 4 + skipped :]
    if pieces > 1:
        assemble_kernel(given, tokens)
    else:
        tokens = given[0]
    weights = (own_in, mate_in), (own_out, mate_out)
    forward_core(tokens, *weights, normed_t, (slope, slope_mate), part, base, total)


def forward(given, count, weights, *earlier):
    width, block = weights[0].shape
    outs = (
        shape((width, count)),
        shape((count, block)),
        shape((count, block)),
        shape((count, width)),
        shape((count, width), f32),
    )
    return pl.pallas_call(
        functools.partial(forward_kernel, len(given), len(earlier)),
        out_shape=outs,
        in_specs=[vmem] * (len(given) + len(weights)) + [anywhere] * len(earlier),
        out_specs=[vmem for out in outs],
        scratch_shapes=[pltpu.VMEM((count, width), f32), pltpu.VMEM((count, width), bf16)],
        compiler_params=limit(12),
        cost_estimate=cost(0, 1000),
    )(*given, *weights, *earlier)


def errors_kernel(base, sent, *refs):
    errors = refs[-1]
    result = base[...] + sent[...].astype(f32)
    rank = lax.broadcasted_iota(jnp.int32, result.shape, 0)
    errors[...] = jnp.where(rank == result.shape[0] - 1, 0.0, result).astype(bf16)


def errors_of(base, sent, *earlier):
    return pl.pallas_call(
        errors_kernel,
        out_shape=shape(base.shape),
        in_specs=[vmem, vmem] + [anywhere] * len(earlier),
        out_specs=vmem,
        compiler_params=limit(2),
        cost_estimate=cost(0, 8 * base.size),
    )(base, sent, *earlier)


def strength_kernel(heat, out):
    out[...] = jnp.sqrt(jnp.full(out.shape, 2.0 * drift_stride * heat[0], f32))


def strength_of(heat, block):
    return pl.pallas_call(
        strength_kernel,
        out_shape=shape((1, block), f32),
        in_specs=[smem],
        out_specs=vmem,
        compiler_params=limit(1),
        cost_estimate=cost(0, 4 * block),
    )(heat)


def hidden_kernel(errors, weight, slope, *refs):
    out = refs[-1]
    tile = min(256, weight.shape[0])
    for at in range(0, weight.shape[0], tile):
        cols = slice(at, at + tile)
        product = against_rows(errors[...], weight[cols]) * slope[:, cols].astype(f32)
        out[:, cols] = product.astype(bf16)


def hidden_of(errors, weight, slope, *earlier):
    count, width = errors.shape
    block = weight.shape[0]
    return pl.pallas_call(
        hidden_kernel,
        out_shape=shape((count, block)),
        in_specs=[vmem] * 3 + [anywhere] * len(earlier),
        out_specs=vmem,
        compiler_params=limit(8),
        cost_estimate=cost(count * width * block, 2 * width * block),
    )(errors, weight, slope, *earlier)


def send_kernel(base, sent, weight, slope, order, errors, grad):
    errors_kernel(base, sent, errors)
    hidden_kernel(errors, weight, slope, grad)


def send_of(base, sent, weight, slope, order):
    count, block = slope.shape
    return pl.pallas_call(
        send_kernel,
        out_shape=(shape(base.shape), shape((count, block))),
        in_specs=[vmem] * 4 + [anywhere],
        out_specs=(vmem, vmem),
        compiler_params=limit(8),
        cost_estimate=cost(base.size * block, 8 * base.size),
    )(base, sent, weight, slope, order)


def carry_kernel(begun, errors, weight, slope, normed, out, grad):
    hidden_kernel(errors, weight, slope, grad)
    width = normed.shape[0]
    rows = width // 4
    scale = drift_stride * width**-0.5
    for start in range(0, width, rows):
        here = slice(start, start + rows)
        out[here] = begun[here] - scale * matmul(normed[here], grad[...])


def carry(begun, errors, weight, slope, normed):
    return pl.pallas_call(
        carry_kernel,
        out_shape=shape(begun.shape, f32),
        in_specs=[vmem] * 5,
        out_specs=vmem,
        scratch_shapes=[pltpu.VMEM(slope.shape, bf16)],
        compiler_params=limit(8),
        cost_estimate=cost(2 * errors.size * slope.shape[1], 8 * begun.size),
    )(begun, errors, weight, slope, normed)


def begin_kernel(strength, first, second, normed, normed_mate, params, noise, out):
    width = params.shape[1]
    rows = width // 4
    for start in range(0, width, rows):
        here = slice(start, start + rows)
        slope = matmul(normed[here], first[...]) + matmul(normed_mate[here], second[...])
        out[here] = (
            (1.0 - drift_stride) * params[0, here].astype(f32)
            + strength[...] * noise[0, here].astype(f32)
            - (drift_stride * width**-0.5) * slope
        )


def begin(strength, grads, normed, params, noise):
    width, count = normed[0].shape
    block = grads[0].shape[1]
    return pl.pallas_call(
        begin_kernel,
        out_shape=shape((width, block), f32),
        in_specs=[vmem] * 7,
        out_specs=vmem,
        compiler_params=limit(4),
        cost_estimate=cost(2 * width * count * block, 8 * width * count),
    )(strength, *grads, *normed, params, noise)


def update_kernel(start, begun, grad, normed, *rest):
    out = rest[-1]
    here = slice(start, start + out.shape[0])
    slope = matmul(normed[here], grad[...])
    out[...] = (begun[here] - (drift_stride * normed.shape[0] ** -0.5) * slope).astype(bf16)


def update(start, rows, begun, grad, normed, *earlier):
    count, block = grad.shape
    return pl.pallas_call(
        functools.partial(update_kernel, start),
        out_shape=shape((rows, block)),
        in_specs=[vmem] * 3 + [anywhere] * len(earlier),
        out_specs=vmem,
        compiler_params=limit(4),
        cost_estimate=cost(rows * count * block, 8 * rows * count),
    )(begun, grad, normed, *earlier)


def role(mate, swapped):
    rank = lax.axis_index("rep")
    odd = rank & 1
    taken = swapped[0] == 1
    return odd, taken & (mate[0] == rank + 1 - 2 * odd), taken & (mate[0] == rank - 1 + 2 * odd)


def finish_kernel(start, stop, count, mate, swapped, *refs):
    own, across, beyond = (refs[i * count : (i + 1) * count] for i in range(3))
    result, gaps, out, done = refs[-4:]
    odd, near_taken, far_taken = role(mate, swapped)
    at = 0
    for mine, near, far in zip(own, across, beyond):
        out[at : at + mine.shape[0]] = jnp.where(
            near_taken, near[...], jnp.where(far_taken, far[...], mine[...])
        )
        at += mine.shape[0]
    copy = pltpu.make_async_copy(out, result.at[0, pl.ds(start, stop - start)], done)
    copy.start()
    near_sum = far_sum = 0.0
    for part in range(count):
        mine, near, far = (pieces[part][...].astype(f32) for pieces in (own, across, beyond))
        near_sum += jnp.sum((near - mine) * (near - mine), axis=0, keepdims=True)
        far_sum += jnp.sum((far - mine) * (far - mine), axis=0, keepdims=True)
    if start > 0:
        so_far = refs[3 * count]
        near_sum += so_far[0, 0:1]
        far_sum += so_far[0, 1:2]
    if stop == result.shape[1]:
        near_sum *= 1.0 / result.shape[1]
        far_sum *= 1.0 / result.shape[1]
        near_sum, far_sum = (
            jnp.where(odd == 1, near_sum, far_sum),
            jnp.where(odd == 1, far_sum, near_sum),
        )
    gaps[0, 0:1] = near_sum
    gaps[0, 1:2] = far_sum
    copy.wait()


def finish(width, start, pairing, own, across, beyond, so_far):
    count = len(own)
    block = own[0].shape[1]
    stop = start + sum(value.shape[0] for value in own)
    given = [*own, *across, *beyond]
    specs = [vmem] * len(given)
    aliases = {}
    if start > 0:
        given += [so_far[1], so_far[0]]
        specs += [vmem, anywhere]
        aliases = {1 + len(given): 0}
    return pl.pallas_call(
        functools.partial(finish_kernel, start, stop, count),
        out_shape=(shape((1, width, block)), shape((1, 2, block), f32)),
        in_specs=[smem, smem] + specs,
        out_specs=(anywhere, vmem),
        scratch_shapes=[pltpu.VMEM((stop - start, block), bf16), pltpu.SemaphoreType.DMA],
        input_output_aliases=aliases,
        compiler_params=limit(4),
        cost_estimate=cost(0, 8 * (stop - start) * block),
    )(*pairing, *given)


def body(
    residual_flow,
    rooted_input_matrix,
    chain_normal_draws,
    output_matrix,
    chain_heat,
    matched_chain,
    swap_mask,
):
    replicas = lax.axis_size("rep")
    params = rooted_input_matrix[0]
    block = params.shape[1]
    count = residual_flow.shape[0]

    def to_core(value):
        return lax.ppermute(value, "dp", [(i, i ^ 1) for i in range(4)])

    def to_chip(value):
        return lax.ppermute(value, "dp", [(i, i ^ 2) for i in range(4)])

    def to_mate(value):
        return lax.ppermute(value, "rep", [(i, i ^ 1) for i in range(replicas)])

    def to_pair(value):
        return lax.ppermute(value, "rep", [(i, i ^ 2) for i in range(replicas)])

    def to_next(value):
        pairs = [(i, (i + (2 if i % 2 == 0 else -2)) % replicas) for i in range(replicas)]
        return lax.ppermute(value, "rep", pairs)

    def to_diagonal(value):
        return lax.ppermute(value, "rep", [(i, i ^ 3) for i in range(replicas)])

    mate_in = to_core(params)
    mate_out = to_core(output_matrix)
    token_share = share(residual_flow)
    token_own = to_chip(token_share)
    weights = (params, mate_in, output_matrix, mate_out)
    normed, slope, slope_send, part, base = forward((residual_flow,), count, weights)
    sent = to_chip(after(part, token_own))
    token_own = after(token_own, part)
    token_pieces = (token_own, to_mate(token_own), to_pair(token_own), to_diagonal(token_own))
    normed_mate = to_core(normed)
    far, far_slope, far_slope_send, far_part, far_base = forward(token_pieces, count, weights)
    far_sent = to_chip(far_part)
    far_mate = to_core(far)

    strength = strength_of(chain_heat, block)
    errors = errors_of(far_base, sent, normed_mate, strength)
    far_grads = [
        hidden_of(errors, output_matrix, far_slope),
        to_core(hidden_of(errors, mate_out, far_slope_send)),
    ]
    begun = begin(
        strength, far_grads, (far, far_mate), rooted_input_matrix, chain_normal_draws
    )
    errors, grad = send_of(base, far_sent, mate_out, slope_send, begun)
    begun = carry(begun, errors, output_matrix, slope, normed)
    grad = to_core(grad)

    pairing = (matched_chain, swap_mask)
    width = params.shape[0]
    sizes = [width * part // 64 for part in (11, 14, 14, 14, 11)]
    starts = [sum(sizes[:chunk]) for chunk in range(len(sizes))]
    fresh = []
    for start, rows in zip(starts, sizes):
        fresh.append(update(start, rows, begun, grad, normed_mate, *fresh[-1:]))
    own, across, beyond = [], [], []
    for chunk, piece in enumerate(fresh):
        earlier = across[chunk - 3 : chunk - 3 + 1] if chunk >= 3 else []
        if chunk == 1:
            earlier = [*earlier, fresh[-1]]
        own.append(after(piece, *earlier) if earlier else piece)
        across.append(to_mate(own[-1]))
    for chunk in range(len(sizes)):
        if chunk >= 2:
            across[chunk] = after(across[chunk], beyond[chunk - 2])
        beyond.append(to_next(across[chunk]))
    done = None
    for first, stop in ((0, 4), (4, 5)):
        given = (pieces[first:stop] for pieces in (own, across, beyond))
        done = finish(width, starts[first], pairing, *given, done)
    return done


def solution(mesh):
    placed = (
        P("dp", None),
        P("rep", None, "dp"),
        P("rep", None, "dp"),
        P("dp", None),
        P("rep"),
        P("rep"),
        P("rep"),
    )
    return jax.shard_map(
        body,
        mesh=mesh,
        in_specs=placed,
        out_specs=(P("rep", None, "dp"), P("rep", None, "dp")),
        check_vma=False,
    )
```

```python
import functools
import math

import jax
import jax.numpy as jnp
from jax import lax
from jax.experimental import pallas as pl
from jax.experimental.pallas import tpu as pltpu
from jax.sharding import PartitionSpec as P

drift_stride = 0.5
f32 = jnp.float32
bf16 = jnp.bfloat16
smem = pl.BlockSpec(memory_space=pltpu.SMEM)


def matmul(left, right):
    return jnp.dot(left, right, preferred_element_type=f32)


def against_rows(left, right):
    return lax.dot_general(left, right, (((1,), (1,)), ((), ())), preferred_element_type=f32)


def limit(mebibytes):
    return pltpu.CompilerParams(vmem_limit_bytes=mebibytes * 1024 * 1024)


def cost(macs, nbytes):
    return pl.CostEstimate(flops=2 * macs, bytes_accessed=nbytes, transcendentals=0)


vmem = pl.BlockSpec(memory_space=pltpu.VMEM)
anywhere = pl.BlockSpec(memory_space=pl.ANY)


def shape(dims, dtype=bf16):
    return jax.ShapeDtypeStruct(dims, dtype)


def after(value, *earlier):
    return pl.pallas_call(
        lambda *refs: None,
        out_shape=shape(value.shape, value.dtype),
        in_specs=[anywhere] * (1 + len(earlier)),
        out_specs=anywhere,
        input_output_aliases={0: 0},
        compiler_params=limit(1),
    )(value, *earlier)


def share_kernel(value, out, done):
    rows = out.shape[0]
    place = lax.axis_index("rep") & 3
    here = pl.ds(pl.multiple_of(place * rows, rows), rows)
    copy = pltpu.make_async_copy(value.at[here], out, done)
    copy.start()
    copy.wait()


def share(value):
    return pl.pallas_call(
        share_kernel,
        out_shape=shape((value.shape[0] // 4, value.shape[1])),
        in_specs=[anywhere],
        out_specs=vmem,
        scratch_shapes=[pltpu.SemaphoreType.DMA],
        compiler_params=limit(1),
        cost_estimate=cost(3 * 10**9, value.size),
    )(value)


def assemble_kernel(pieces, out):
    rows = pieces[0].shape[0]
    for place in range(4):

        @pl.when((lax.axis_index("rep") & 3) == place)
        def _():
            for at, piece in enumerate(pieces):
                out[(place ^ at) * rows : ((place ^ at) + 1) * rows] = piece[...]


def normalized(tokens):
    values = tokens.astype(f32)
    center = values - jnp.mean(values, axis=1, keepdims=True)
    spread = jnp.mean(center * center, axis=1, keepdims=True)
    return (center * lax.rsqrt(spread + 1e-05)).astype(bf16)


def gelu_both(values):
    coeff = math.sqrt(2.0 / math.pi)
    square = values * values
    gate = 0.5 + 0.5 * jnp.tanh(coeff * values * (1.0 + 0.044715 * square))
    hidden = values * gate
    slope = gate + hidden * (1.0 - gate) * (2.0 * coeff + 6.0 * 0.044715 * coeff * square)
    return hidden.astype(bf16), slope.astype(bf16)


def forward_core(tokens, weights_in, weights_out, normed_t, slopes, part, base, total):
    count, width = tokens.shape
    block = weights_in[0].shape[1]
    tile = min(256, block)
    normed = normalized(tokens[...])
    normed_t[...] = normed.T
    for side in range(2):
        for at in range(0, block, tile):
            values = matmul(normed, weights_in[side][:, at : at + tile]) * (width**-0.5)
            hidden, slopes[side][:, at : at + tile] = gelu_both(values)
            term = matmul(hidden, weights_out[side][at : at + tile])
            if side + at == 0:
                total[...] = term
            else:
                total[...] += term
    part[...] = total[...].astype(bf16)
    values = tokens[...].astype(f32)
    ahead = pltpu.roll(values, count - 1, 0)
    rank = lax.broadcasted_iota(jnp.int32, values.shape, 0)
    base[...] = jnp.where(rank == count - 1, 0.0, total[...] + values - ahead)


def forward_kernel(pieces, skipped, *refs):
    given = refs[:pieces]
    own_in, mate_in, own_out, mate_out = refs[pieces : pieces + 4]
    normed_t, slope, slope_mate, part, base, total, tokens = refs[pieces + 4 + skipped :]
    if pieces > 1:
        assemble_kernel(given, tokens)
    else:
        tokens = given[0]
    weights = (own_in, mate_in), (own_out, mate_out)
    forward_core(tokens, *weights, normed_t, (slope, slope_mate), part, base, total)


def forward(given, count, weights, *earlier):
    width, block = weights[0].shape
    outs = (
        shape((width, count)),
        shape((count, block)),
        shape((count, block)),
        shape((count, width)),
        shape((count, width), f32),
    )
    return pl.pallas_call(
        functools.partial(forward_kernel, len(given), len(earlier)),
        out_shape=outs,
        in_specs=[vmem] * (len(given) + len(weights)) + [anywhere] * len(earlier),
        out_specs=[vmem for out in outs],
        scratch_shapes=[pltpu.VMEM((count, width), f32), pltpu.VMEM((count, width), bf16)],
        compiler_params=limit(12),
        cost_estimate=cost(0, 1000),
    )(*given, *weights, *earlier)


def errors_kernel(base, sent, *refs):
    errors = refs[-1]
    result = base[...] + sent[...].astype(f32)
    rank = lax.broadcasted_iota(jnp.int32, result.shape, 0)
    errors[...] = jnp.where(rank == result.shape[0] - 1, 0.0, result).astype(bf16)


def errors_of(base, sent, *earlier):
    return pl.pallas_call(
        errors_kernel,
        out_shape=shape(base.shape),
        in_specs=[vmem, vmem] + [anywhere] * len(earlier),
        out_specs=vmem,
        compiler_params=limit(2),
        cost_estimate=cost(0, 8 * base.size),
    )(base, sent, *earlier)


def strength_kernel(heat, out):
    out[...] = jnp.sqrt(jnp.full(out.shape, 2.0 * drift_stride * heat[0], f32))


def strength_of(heat, block):
    return pl.pallas_call(
        strength_kernel,
        out_shape=shape((1, block), f32),
        in_specs=[smem],
        out_specs=vmem,
        compiler_params=limit(1),
        cost_estimate=cost(0, 4 * block),
    )(heat)


def hidden_kernel(errors, weight, slope, *refs):
    out = refs[-1]
    tile = min(256, weight.shape[0])
    for at in range(0, weight.shape[0], tile):
        cols = slice(at, at + tile)
        product = against_rows(errors[...], weight[cols]) * slope[:, cols].astype(f32)
        out[:, cols] = product.astype(bf16)


def hidden_of(errors, weight, slope, *earlier):
    count, width = errors.shape
    block = weight.shape[0]
    return pl.pallas_call(
        hidden_kernel,
        out_shape=shape((count, block)),
        in_specs=[vmem] * 3 + [anywhere] * len(earlier),
        out_specs=vmem,
        compiler_params=limit(8),
        cost_estimate=cost(count * width * block, 2 * width * block),
    )(errors, weight, slope, *earlier)


def send_kernel(base, sent, weight, slope, order, errors, grad):
    errors_kernel(base, sent, errors)
    hidden_kernel(errors, weight, slope, grad)


def send_of(base, sent, weight, slope, order):
    count, block = slope.shape
    return pl.pallas_call(
        send_kernel,
        out_shape=(shape(base.shape), shape((count, block))),
        in_specs=[vmem] * 4 + [anywhere],
        out_specs=(vmem, vmem),
        compiler_params=limit(8),
        cost_estimate=cost(base.size * block, 8 * base.size),
    )(base, sent, weight, slope, order)


def carry_kernel(begun, errors, weight, slope, normed, out, grad):
    hidden_kernel(errors, weight, slope, grad)
    width = normed.shape[0]
    rows = width // 4
    scale = drift_stride * width**-0.5
    for start in range(0, width, rows):
        here = slice(start, start + rows)
        out[here] = begun[here] - scale * matmul(normed[here], grad[...])


def carry(begun, errors, weight, slope, normed):
    return pl.pallas_call(
        carry_kernel,
        out_shape=shape(begun.shape, f32),
        in_specs=[vmem] * 5,
        out_specs=vmem,
        scratch_shapes=[pltpu.VMEM(slope.shape, bf16)],
        compiler_params=limit(8),
        cost_estimate=cost(2 * errors.size * slope.shape[1], 8 * begun.size),
    )(begun, errors, weight, slope, normed)


def begin_kernel(strength, first, second, normed, normed_mate, params, noise, out):
    width = params.shape[1]
    rows = width // 4
    for start in range(0, width, rows):
        here = slice(start, start + rows)
        slope = matmul(normed[here], first[...]) + matmul(normed_mate[here], second[...])
        out[here] = (
            (1.0 - drift_stride) * params[0, here].astype(f32)
            + strength[...] * noise[0, here].astype(f32)
            - (drift_stride * width**-0.5) * slope
        )


def begin(strength, grads, normed, params, noise):
    width, count = normed[0].shape
    block = grads[0].shape[1]
    return pl.pallas_call(
        begin_kernel,
        out_shape=shape((width, block), f32),
        in_specs=[vmem] * 7,
        out_specs=vmem,
        compiler_params=limit(4),
        cost_estimate=cost(2 * width * count * block, 8 * width * count),
    )(strength, *grads, *normed, params, noise)


def update_kernel(start, begun, grad, normed, *rest):
    out = rest[-1]
    here = slice(start, start + out.shape[0])
    slope = matmul(normed[here], grad[...])
    out[...] = (begun[here] - (drift_stride * normed.shape[0] ** -0.5) * slope).astype(bf16)


def update(start, rows, begun, grad, normed, *earlier):
    count, block = grad.shape
    return pl.pallas_call(
        functools.partial(update_kernel, start),
        out_shape=shape((rows, block)),
        in_specs=[vmem] * 3 + [anywhere] * len(earlier),
        out_specs=vmem,
        compiler_params=limit(4),
        cost_estimate=cost(rows * count * block, 8 * rows * count),
    )(begun, grad, normed, *earlier)


def role(mate, swapped):
    rank = lax.axis_index("rep")
    odd = rank & 1
    taken = swapped[0] == 1
    return odd, taken & (mate[0] == rank + 1 - 2 * odd), taken & (mate[0] == rank - 1 + 2 * odd)


def finish_kernel(start, stop, count, mate, swapped, *refs):
    own, across, beyond = (refs[i * count : (i + 1) * count] for i in range(3))
    result, gaps, out, done = refs[-4:]
    odd, near_taken, far_taken = role(mate, swapped)
    at = 0
    for mine, near, far in zip(own, across, beyond):
        out[at : at + mine.shape[0]] = jnp.where(
            near_taken, near[...], jnp.where(far_taken, far[...], mine[...])
        )
        at += mine.shape[0]
    copy = pltpu.make_async_copy(out, result.at[0, pl.ds(start, stop - start)], done)
    copy.start()
    near_sum = far_sum = 0.0
    for part in range(count):
        mine, near, far = (pieces[part][...].astype(f32) for pieces in (own, across, beyond))
        near_sum += jnp.sum((near - mine) * (near - mine), axis=0, keepdims=True)
        far_sum += jnp.sum((far - mine) * (far - mine), axis=0, keepdims=True)
    if start > 0:
        so_far = refs[3 * count]
        near_sum += so_far[0, 0:1]
        far_sum += so_far[0, 1:2]
    if stop == result.shape[1]:
        near_sum *= 1.0 / result.shape[1]
        far_sum *= 1.0 / result.shape[1]
        near_sum, far_sum = (
            jnp.where(odd == 1, near_sum, far_sum),
            jnp.where(odd == 1, far_sum, near_sum),
        )
    gaps[0, 0:1] = near_sum
    gaps[0, 1:2] = far_sum
    copy.wait()


def finish(width, start, pairing, own, across, beyond, so_far):
    count = len(own)
    block = own[0].shape[1]
    stop = start + sum(value.shape[0] for value in own)
    given = [*own, *across, *beyond]
    specs = [vmem] * len(given)
    aliases = {}
    if start > 0:
        given += [so_far[1], so_far[0]]
        specs += [vmem, anywhere]
        aliases = {1 + len(given): 0}
    return pl.pallas_call(
        functools.partial(finish_kernel, start, stop, count),
        out_shape=(shape((1, width, block)), shape((1, 2, block), f32)),
        in_specs=[smem, smem] + specs,
        out_specs=(anywhere, vmem),
        scratch_shapes=[pltpu.VMEM((stop - start, block), bf16), pltpu.SemaphoreType.DMA],
        input_output_aliases=aliases,
        compiler_params=limit(4),
        cost_estimate=cost(0, 8 * (stop - start) * block),
    )(*pairing, *given)


def body(
    residual_flow,
    rooted_input_matrix,
    chain_normal_draws,
    output_matrix,
    chain_heat,
    matched_chain,
    swap_mask,
):
    replicas = lax.axis_size("rep")
    params = rooted_input_matrix[0]
    block = params.shape[1]
    count = residual_flow.shape[0]

    def to_core(value):
        return lax.ppermute(value, "dp", [(i, i ^ 1) for i in range(4)])

    def to_chip(value):
        return lax.ppermute(value, "dp", [(i, i ^ 2) for i in range(4)])

    def to_mate(value):
        return lax.ppermute(value, "rep", [(i, i ^ 1) for i in range(replicas)])

    def to_pair(value):
        return lax.ppermute(value, "rep", [(i, i ^ 2) for i in range(replicas)])

    def to_next(value):
        pairs = [(i, (i + (2 if i % 2 == 0 else -2)) % replicas) for i in range(replicas)]
        return lax.ppermute(value, "rep", pairs)

    def to_diagonal(value):
        return lax.ppermute(value, "rep", [(i, i ^ 3) for i in range(replicas)])

    mate_in = to_core(params)
    mate_out = to_core(output_matrix)
    token_share = share(residual_flow)
    token_own = to_chip(token_share)
    weights = (params, mate_in, output_matrix, mate_out)
    normed, slope, slope_send, part, base = forward((residual_flow,), count, weights)
    sent = to_chip(after(part, token_own))
    token_own = after(token_own, part)
    token_pieces = (token_own, to_mate(token_own), to_pair(token_own), to_diagonal(token_own))
    normed_mate = to_core(normed)
    far, far_slope, far_slope_send, far_part, far_base = forward(token_pieces, count, weights)
    far_sent = to_chip(far_part)
    far_mate = to_core(far)

    strength = strength_of(chain_heat, block)
    errors = errors_of(far_base, sent, normed_mate, strength)
    far_grads = [
        hidden_of(errors, output_matrix, far_slope),
        to_core(hidden_of(errors, mate_out, far_slope_send)),
    ]
    begun = begin(
        strength, far_grads, (far, far_mate), rooted_input_matrix, chain_normal_draws
    )
    errors, grad = send_of(base, far_sent, mate_out, slope_send, begun)
    begun = carry(begun, errors, output_matrix, slope, normed)
    grad = to_core(grad)

    pairing = (matched_chain, swap_mask)
    width = params.shape[0]
    sizes = [width * part // 64 for part in (11, 14, 14, 14, 11)]
    starts = [sum(sizes[:chunk]) for chunk in range(len(sizes))]
    fresh = []
    for start, rows in zip(starts, sizes):
        fresh.append(update(start, rows, begun, grad, normed_mate, *fresh[-1:]))
    own, across, beyond = [], [], []
    for chunk, piece in enumerate(fresh):
        earlier = across[chunk - 3 : chunk - 3 + 1] if chunk >= 3 else []
        if chunk == 1:
            earlier = [*earlier, fresh[-1]]
        own.append(after(piece, *earlier) if earlier else piece)
        across.append(to_mate(own[-1]))
    for chunk in range(len(sizes)):
        if chunk >= 2:
            across[chunk] = after(across[chunk], beyond[chunk - 2])
        beyond.append(to_next(across[chunk]))
    done = None
    for first, stop in ((0, 3), (3, 4), (4, 5)):
        given = (pieces[first:stop] for pieces in (own, across, beyond))
        done = finish(width, starts[first], pairing, *given, done)
    return done


def solution(mesh):
    placed = (
        P("dp", None),
        P("rep", None, "dp"),
        P("rep", None, "dp"),
        P("dp", None),
        P("rep"),
        P("rep"),
        P("rep"),
    )
    return jax.shard_map(
        body,
        mesh=mesh,
        in_specs=placed,
        out_specs=(P("rep", None, "dp"), P("rep", None, "dp")),
        check_vma=False,
    )
```
